512 devices in a mesh: gx: 32 (over y, x, core), gy: 16 (over z).
Axes of the slice: x: 4, y: 4, z: 16, core: 2. Of those that a mesh axis runs over, the one named last changes fastest.
Arguments:
- field: float32 [1024, 512, 384], P('gx', 'gy'), may hold values from -6 to 6
- vertical: float32 [3, 6, 64, 64], replicated, may hold values from -0.75 to 0.75
- horiz_kernel: float32 [3, 2, 6, 9], replicated, may hold values from 0.05 to 1
- gen_weight: float32 [3, 6], replicated, may hold values from 0.3 to 1.5
Outputs:
- covaried: float32 [1024, 512, 384], P('gx', 'gy')
The draws below stay inside these ranges and needn't reach their ends.
All inputs are finite; a program needn't handle non-finite values.
Results may differ from the reference program's by a relative error of at most 0.0001.
Values sent between devices are 32-bit elements; how exact they have to be, the bound alone decides.
A program may use at most 64 MiB of HBM per device.

```python
import math
import jax
import jax.numpy as jnp
from jax import lax

V = 6
NZ = 64
GENS = 2
HALF = 4
TAPS = 9
NX = 1024
NY = 512


def block_scale(own_key, shape, cuts, low, high):
    level = 1.0
    for axis_at, shards_of in cuts:
        steps = jax.random.uniform(jax.random.fold_in(jax.random.fold_in(own_key, 6), axis_at), (shards_of,), jnp.float32, low / len(cuts), high / len(cuts))
        level = level * jnp.repeat(jnp.exp(steps), shape[axis_at] // shards_of).reshape((-1,) + (1,) * (len(shape) - 1 - axis_at))
    return level


def noise(own_key, dims, deviation, bound, split=(), kind=jnp.bfloat16):
    loudness = block_scale(own_key, dims, split, -0.22, 0.18) if split else 1.0
    drawn = jax.random.normal(own_key, dims, jnp.float32) * deviation * loudness
    return jnp.minimum(jnp.maximum(drawn, -bound), bound).astype(kind)


def setup_inputs(seed: int = 0) -> dict:
    key_of = jax.random.split(jax.random.key(seed), 5)
    return {
        "field": noise(key_of[0], (NX, NY, V * NZ), 1.0, 6.0, ((0, 32), (1, 16)), jnp.float32),
        "vertical": noise(key_of[1], (GENS + 1, V, NZ, NZ), NZ ** -0.5, 0.75, (), jnp.float32),
        "horiz_kernel": jnp.clip(jnp.exp(jax.random.uniform(key_of[2], (GENS + 1, 2, V, TAPS), jnp.float32, math.log(0.05), math.log(1.0))), 0.05, 1.0),
        "gen_weight": jnp.clip(jnp.exp(jax.random.uniform(key_of[3], (GENS + 1, V), jnp.float32, math.log(0.3), math.log(1.5))), 0.3, 1.5),
    }


def taps_along(grid, kern, axis):
    count = grid.shape[axis]
    pads = [(0, 0)] * grid.ndim
    pads[axis] = (HALF, HALF)
    padded = jnp.pad(grid, pads)
    total = jnp.zeros_like(grid)
    for step in range(2 * HALF + 1):
        total = total + kern[step] * lax.slice_in_dim(padded, step, step + count, axis=axis)
    return total


def coarsen(grid):
    nrow, ncol, nlev = grid.shape
    return grid.reshape(nrow // 2, 2, ncol // 2, 2, nlev).mean(axis=(1, 3))


def refine(grid):
    return jnp.repeat(jnp.repeat(grid, 2, axis=0), 2, axis=1)


def one_variable(inputs):
    grid, matrices, kernels, weights = inputs
    norms = kernels / jnp.sum(kernels, axis=-1, keepdims=True)
    filtered = []
    current = grid
    for level in range(GENS + 1):
        if level > 0:
            current = coarsen(current)
        along_x = taps_along(current, norms[level, 0], 0)
        along_y = taps_along(along_x, norms[level, 1], 1)
        filtered.append(jnp.einsum("abz,zw->abw", along_y, matrices[level], precision=lax.Precision.HIGHEST))
    total = weights[GENS] * filtered[GENS]
    for level in range(GENS - 1, -1, -1):
        total = weights[level] * filtered[level] + refine(total)
    return total


def reference(field, vertical, horiz_kernel, gen_weight):
    grids = field.reshape(NX, NY, V, NZ).transpose(2, 0, 1, 3)
    result = lax.map(one_variable, (grids, vertical.transpose(1, 0, 2, 3), horiz_kernel.transpose(2, 0, 1, 3), gen_weight.T))
    return result.transpose(1, 2, 0, 3).reshape(NX, NY, V * NZ)
```

```python
import functools

import jax
import jax.numpy as jnp
from jax import lax
from jax.experimental import pallas as pl
from jax.experimental.pallas import tpu as pltpu
from jax.sharding import PartitionSpec as P

GENS = 3
HALF = 4
TAPS = 9
VARS = 6
LEVELS = 64
LANES = 128
GROUPS = 3
MESH = pl.DeviceIdType.MESH
F32 = jnp.float32
BF16 = jnp.bfloat16


def line_sum(pieces, taps):
    total = taps[0] * pieces[0]
    for step in range(1, TAPS):
        total = total + taps[step] * pieces[step]
    return total


def kernel(nx, ny, field, vertical, horiz, weight, out,
           grid0, grid1, grid2, side0, side1, side2, wide0, wide1, wide2,
           vert, hk, gw, taps, wfull, mats, pair, left0, left1, left2, up1, up2,
           load_sem, send_sem, recv_sem):
    gx, gy = lax.axis_index("gx"), lax.axis_index("gy")
    grids, sides, wides = (grid0, grid1, grid2), (side0, side1, side2), (wide0, wide1, wide2)
    sizes = (32, 16, 8)

    loads = [
        pltpu.make_async_copy(
            field.at[:, :, pl.ds(g * LANES, LANES)], grid0.at[g, pl.ds(HALF, 32)], load_sem.at[g])
        for g in range(GROUPS)
    ]
    for n, (src, dst) in enumerate(((vertical, vert), (horiz, hk), (weight, gw))):
        loads.append(pltpu.make_async_copy(src, dst, load_sem.at[GROUPS + n]))
    for load in loads:
        load.start()

    has = {"xl": gx > 0, "xr": gx < nx - 1, "zl": gy > 0, "zr": gy < ny - 1}
    ids = {"xl": {"gx": gx - 1}, "xr": {"gx": gx + 1}, "zl": {"gy": gy - 1}, "zr": {"gy": gy + 1}}
    back = {"xl": "xr", "xr": "xl", "zl": "zr", "zr": "zl"}

    barrier = pltpu.get_barrier_semaphore()
    for way in has:
        @pl.when(has[way])
        def _(way=way):
            pl.semaphore_signal(barrier, inc=1, device_id=ids[way], device_id_type=MESH)

    for way in has:
        @pl.when(jnp.logical_not(has[way]))
        def _(way=way):
            for grid, side, size in zip(grids, sides, sizes):
                if way == "xl":
                    grid[:, 0:HALF] = jnp.zeros((GROUPS, HALF, size, LANES), F32)
                    side[:, 0:HALF] = jnp.zeros((GROUPS, HALF, 8, LANES), F32)
                elif way == "xr":
                    grid[:, size + HALF:] = jnp.zeros((GROUPS, HALF, size, LANES), F32)
                    side[:, size + HALF:] = jnp.zeros((GROUPS, HALF, 8, LANES), F32)
                else:
                    at = HALF if way == "zl" else 0
                    side[:, HALF:size + HALF, at:at + HALF] = jnp.zeros((GROUPS, size, HALF, LANES), F32)

    copies = {}

    def add(name, way, src, dst):
        slot = len(copies)
        copies[name] = (way, pltpu.make_async_remote_copy(
            src_ref=src, dst_ref=dst, send_sem=send_sem.at[slot], recv_sem=recv_sem.at[slot],
            device_id=ids[way], device_id_type=MESH))

    every = pl.ds(0, GROUPS)
    for level, size in enumerate(sizes):
        grid, side = grids[level], sides[level]
        low, high = pl.ds(HALF, HALF), pl.ds(size, HALF)
        add(("x", level, "xl"), "xl", grid.at[:, low], grid.at[:, pl.ds(size + HALF, HALF)])
        add(("x", level, "xr"), "xr", grid.at[:, high], grid.at[:, pl.ds(0, HALF)])
        add(("c", level, "xl"), "xl", side.at[:, low], side.at[:, pl.ds(size + HALF, HALF)])
        add(("c", level, "xr"), "xr", side.at[:, high], side.at[:, pl.ds(0, HALF)])
        for way, here, there in (("zl", 0, 0), ("zr", size - HALF, HALF)):
            cols, to = pl.ds(here, HALF), pl.ds(there, HALF)
            if level == 2:
                rows = pl.ds(HALF, size)
                add(("z", level, "lo", way), way, grid.at[:, rows, cols], side.at[:, rows, to])
            else:
                add(("z", level, "lo", way), way, grid.at[:, low, cols], side.at[:, low, to])
                add(("z", level, "hi", way), way, grid.at[:, high, cols], side.at[:, high, to])
                rows = pl.ds(2 * HALF, size - 2 * HALF)
                for g in range(GROUPS):
                    add(("z", level, g, way), way, grid.at[g, rows, cols], side.at[g, rows, to])

    def each(names, act):
        by_way = {}
        for name in names:
            by_way.setdefault(name[-1], []).append(name)
        for way, group in by_way.items():
            gate = has[back[way]] if act == "wait_recv" else has[way]

            @pl.when(gate)
            def _(group=group):
                for name in group:
                    getattr(copies[name][1], act)()

    xs, zs = ("xl", "xr"), ("zl", "zr")
    for g in range(GROUPS):
        loads[g].wait()
    pl.semaphore_wait(barrier, sum(flag.astype(jnp.int32) for flag in has.values()))

    first = [("z", 0, end, way) for end in ("lo", "hi") for way in zs] + [("x", 0, way) for way in xs]
    each(first, "start")

    def coarsen(g, carry):
        for fine, coarse, size in ((grid0, grid1, 16), (grid1, grid2, 8)):
            def rows(r, c):
                base = HALF + 2 * r
                pair[r, 0:2 * size] = fine[g, base] + fine[g, base + 1]
                coarse[g, HALF + r] = 0.25 * (
                    pair[r, pl.ds(0, size, stride=2)] + pair[r, pl.ds(1, size, stride=2)])
                return c
            lax.fori_loop(0, size, rows, 0, unroll=True)
        return carry

    lax.fori_loop(0, GROUPS, coarsen, 0)

    second = [("z", 1, "lo", way) for way in zs] + [("z", 1, "hi", way) for way in zs]
    second += [("z", 2, "lo", way) for way in zs]
    second += [("x", level, way) for level in (1, 2) for way in xs]
    each(second, "start")
    third = [("z", level, g, way) for g in range(GROUPS) for level in (0, 1) for way in zs]
    each(third, "start")

    for load in loads[GROUPS:]:
        load.wait()
    lane = lax.broadcasted_iota(jnp.int32, (VARS, GROUPS * LANES), 1)
    row = lax.broadcasted_iota(jnp.int32, (VARS, GROUPS * LANES), 0)
    pick = jnp.where((lane >= row * LEVELS) & (lane < (row + 1) * LEVELS), 1.0, 0.0).astype(F32)
    for level in range(GENS):
        for axis in range(2):
            norm = hk[level, axis] / jnp.sum(hk[level, axis], axis=-1, keepdims=True)
            spread = lax.dot_general(norm, pick, (((0,), (0,)), ((), ())),
                                     precision=lax.Precision.HIGHEST, preferred_element_type=F32)
            for g in range(GROUPS):
                taps[level, axis, g, 0:TAPS] = spread[:, g * LANES:(g + 1) * LANES]
    scale = jnp.dot(gw[...], pick, precision=lax.Precision.HIGHEST, preferred_element_type=F32)
    wfull[...] = jnp.zeros_like(wfull)
    for level in range(GENS):
        for g in range(GROUPS):
            wfull[0:LEVELS, 0:LEVELS] = vert[level, 2 * g]
            wfull[LEVELS:LANES, LEVELS:LANES] = vert[level, 2 * g + 1]
            whole = wfull[...] * scale[level:level + 1, g * LANES:(g + 1) * LANES]
            head = whole.astype(BF16)
            tail = (whole - head.astype(F32)).astype(BF16)
            for at in (0, LANES):
                mats[level, g, at:at + LANES, 0:LANES] = head
                mats[level, g, at:at + LANES, LANES:] = tail

    def taps_of(level, axis, g):
        return [taps[level, axis, g, step:step + 1] for step in range(TAPS)]

    def along_x(source, g, r, cols, ktaps):
        block = source[g, pl.ds(r, 16), cols]
        return line_sum([block[step:step + 8] for step in range(TAPS)], ktaps)

    each([("x", 0, way) for way in xs], "wait_recv")

    def own_x(level, g):
        size = sizes[level]
        ktaps = taps_of(level, 0, g)

        def rows(n, carry):
            r = n * 8
            for t in range(size // 8):
                wides[level][g, pl.ds(r, 8), 8 + 8 * t:16 + 8 * t] = along_x(
                    grids[level], g, r, pl.ds(8 * t, 8), ktaps)
            return carry

        lax.fori_loop(0, size // 8, rows, 0)

    def own0(g, carry):
        own_x(0, g)
        return carry

    lax.fori_loop(0, GROUPS, own0, 0)

    each([("z", level, end, way) for level in (0, 1) for end in ("lo", "hi") for way in zs]
         + [("z", 2, "lo", way) for way in zs], "wait_recv")
    corners = [("c", level, way) for level in range(GENS) for way in xs]
    each(corners, "start")

    each([("x", level, way) for level in (1, 2) for way in xs], "wait_recv")

    def own12(g, carry):
        own_x(1, g)
        own_x(2, g)
        return carry

    lax.fori_loop(0, GROUPS, own12, 0)
    each(corners, "wait_recv")

    for g in range(GROUPS):
        each([("z", level, g, way) for level in (0, 1) for way in zs], "wait_recv")
        for level in (2, 1, 0):
            size, side, wide = sizes[level], sides[level], wides[level]
            left = (left0, left1, left2)[level]
            kx, ky = taps_of(level, 0, g), taps_of(level, 1, g)
            tiles = size // 8

            def rows(n, carry):
                r = n * 8 if isinstance(n, int) else pl.multiple_of(n * 8, 8)
                halo = along_x(side, g, r, pl.ds(0, 8), kx)
                wide[g, pl.ds(r, 8), 0:8] = halo
                wide[g, pl.ds(r, 8), size + 8:size + 16] = halo
                for t in range(tiles):
                    mixed = line_sum(
                        [wide[g, pl.ds(r, 8), 8 * t + HALF + step:8 * t + HALF + step + 8] for step in range(TAPS)],
                        ky).reshape(64, LANES)
                    head = mixed.astype(BF16)
                    tail = (mixed - head.astype(F32)).astype(BF16)
                    at = pl.ds(n * (64 * tiles) + 64 * t, 64)
                    left[at, 0:LANES] = head
                    left[at, LANES:] = tail
                return carry

            lax.fori_loop(0, size // 8, rows, 0)

            def product(n, carry):
                both = jnp.dot(left[pl.ds(n * (64 * tiles), 64 * tiles)], mats[level, g],
                               preferred_element_type=F32)
                total = both[:, 0:LANES] + both[:, LANES:]
                for t in range(tiles):
                    part = total[64 * t:64 * t + 64].reshape(8, 8, LANES)
                    if level < 2:
                        coarse = (up1, up2)[level][pl.ds(n * 4, 4), 8 * t:8 * t + 8]
                        part = part + jnp.broadcast_to(coarse[:, None], (4, 2, 8, LANES)).reshape(8, 8, LANES)
                    if level == 0:
                        out[pl.ds(n * 8, 8), 8 * t:8 * t + 8, g * LANES:(g + 1) * LANES] = part
                    else:
                        finer = (up1, up2)[level - 1]
                        for i in range(8):
                            for odd in range(2):
                                finer[n * 8 + i, pl.ds(16 * t + odd, 8, stride=2)] = part[i]
                return carry

            lax.fori_loop(0, size // 8, product, 0)

    each(list(copies), "wait_send")


def solution(mesh):
    nx, ny = mesh.shape["gx"], mesh.shape["gy"]

    def body(field, vertical, horiz_kernel, gen_weight):
        vmem = pltpu.VMEM
        return pl.pallas_call(
            functools.partial(kernel, nx, ny),
            out_shape=jax.ShapeDtypeStruct(field.shape, F32),
            in_specs=[pl.BlockSpec(memory_space=pltpu.MemorySpace.HBM)] * 4,
            out_specs=pl.BlockSpec(memory_space=pltpu.MemorySpace.VMEM),
            scratch_shapes=[
                vmem((GROUPS, 40, 32, LANES), F32),
                vmem((GROUPS, 24, 16, LANES), F32),
                vmem((GROUPS, 16, 8, LANES), F32),
                vmem((GROUPS, 40, 8, LANES), F32),
                vmem((GROUPS, 24, 8, LANES), F32),
                vmem((GROUPS, 16, 8, LANES), F32),
                vmem((GROUPS, 32, 48, LANES), F32),
                vmem((GROUPS, 16, 32, LANES), F32),
                vmem((GROUPS, 8, 24, LANES), F32),
                vmem(vertical.shape, F32),
                vmem(horiz_kernel.shape, F32),
                vmem(gen_weight.shape, F32),
                vmem((GENS, 2, GROUPS, 16, LANES), F32),
                vmem((LANES, LANES), F32),
                vmem((GENS, GROUPS, 2 * LANES, 2 * LANES), BF16),
                vmem((16, 32, LANES), F32),
                vmem((1024, 2 * LANES), BF16),
                vmem((256, 2 * LANES), BF16),
                vmem((64, 2 * LANES), BF16),
                vmem((16, 32, LANES), F32),
                vmem((8, 16, LANES), F32),
                pltpu.SemaphoreType.DMA((GROUPS + 3,)),
                pltpu.SemaphoreType.DMA((34,)),
                pltpu.SemaphoreType.DMA((34,)),
            ],
            compiler_params=pltpu.CompilerParams(
                collective_id=0, has_side_effects=True, vmem_limit_bytes=40 * 2 ** 20),
        )(field, vertical, horiz_kernel, gen_weight)

    return jax.shard_map(
        body, mesh=mesh, in_specs=(P("gx", "gy", None), P(), P(), P()),
        out_specs=P("gx", "gy", None), check_vma=False)
```

```python
import functools

import jax
import jax.numpy as jnp
from jax import lax
from jax.experimental import pallas as pl
from jax.experimental.pallas import tpu as pltpu
from jax.sharding import PartitionSpec as P

GENS = 3
HALF = 4
TAPS = 9
VARS = 6
LEVELS = 64
LANES = 128
GROUPS = 3
SIZES = (32, 16, 8)
MESH = pl.DeviceIdType.MESH
F32 = jnp.float32
BF16 = jnp.bfloat16

BELOW, LOW, HIGH, MIDDLE, ABOVE, ROWS = 0, 12, 24, 36, 68, 80
UNITS = (
    (0, 12, 36, 40, 44, 48, 52, 56, 24, 68),
    (4, 16, 60, 64, 28, 72),
    (8, 20, 32, 76),
)


def line_sum(pieces, taps):
    total = taps[0] * pieces[0]
    for piece, tap in zip(pieces[1:], taps[1:]):
        total = total + tap * piece
    return total


def split_into(ref, at, values):
    rows = values.shape[0] * values.shape[1]
    flat = values.reshape(rows, LANES)
    head = flat.astype(BF16)
    ref[at:at + rows, 0:LANES] = head
    ref[at:at + rows, LANES:] = (flat - head.astype(F32)).astype(BF16)


def kernel(nx, ny, field, vertical, horiz, weight, out,
           grid0, grid1, grid2, send, halo, wide0a, wide0b, wide1a, wide1b, wide2,
           vert, hk, gw, taps, coef, wfull, mats, pair,
           left0a, left0b, left1a, left1b, left2, twice, left_edge, part1, part2, up1, up2,
           load_sem, send_sem, recv_sem):
    gx, gy = lax.axis_index("gx"), lax.axis_index("gy")
    grids = (grid0, grid1, grid2)

    loads = [
        pltpu.make_async_copy(
            field.at[:, :, pl.ds(g * LANES, LANES)], grid0.at[g, pl.ds(HALF, 32)], load_sem.at[g])
        for g in range(GROUPS)
    ]
    for n, (src, dst) in enumerate(((vertical, vert), (horiz, hk), (weight, gw))):
        loads.append(pltpu.make_async_copy(src, dst, load_sem.at[GROUPS + n]))
    for load in loads:
        load.start()

    has = {"xl": gx > 0, "xr": gx < nx - 1, "zl": gy > 0, "zr": gy < ny - 1}
    ids = {"xl": {"gx": gx - 1}, "xr": {"gx": gx + 1}, "zl": {"gy": gy - 1}, "zr": {"gy": gy + 1}}
    back = {"xl": "xr", "xr": "xl", "zl": "zr", "zr": "zl"}
    xs, zs = ("xl", "xr"), ("zl", "zr")

    barrier = pltpu.get_barrier_semaphore()
    for way in has:
        @pl.when(has[way])
        def _(way=way):
            pl.semaphore_signal(barrier, inc=1, device_id=ids[way], device_id_type=MESH)

    for way in has:
        @pl.when(jnp.logical_not(has[way]))
        def _(way=way):
            if way in xs:
                for grid, size in zip(grids, SIZES):
                    at = 0 if way == "xl" else size + HALF
                    grid[:, at:at + HALF] = jnp.zeros((GROUPS, HALF, size, LANES), F32)
                at = BELOW if way == "xl" else ABOVE
                halo[:, at:at + 12] = jnp.zeros((GROUPS, 12, 8, LANES), F32)
            else:
                at = HALF if way == "zl" else 0
                halo[:, LOW:ABOVE, at:at + HALF] = jnp.zeros((GROUPS, ABOVE - LOW, HALF, LANES), F32)
    for wide, size in ((wide0a, 32), (wide0b, 32), (wide1a, 16), (wide1b, 16), (wide2, 8)):
        wide[:, 0:8] = jnp.zeros((8, 8, LANES), F32)
        wide[:, size + 8:] = jnp.zeros((8, 8, LANES), F32)

    def remote(way, src, dst, slot):
        return pltpu.make_async_remote_copy(
            src_ref=src, dst_ref=dst, send_sem=send_sem.at[slot], recv_sem=recv_sem.at[slot],
            device_id=ids[way], device_id_type=MESH)

    def x_copy(way, level):
        grid, size = grids[level], SIZES[level]
        here, there = (HALF, size + HALF) if way == "xl" else (size, 0)
        return remote(way, grid.at[:, pl.ds(here, HALF)], grid.at[:, pl.ds(there, HALF)],
                      level * 2 + xs.index(way))

    def z_copy(way, part, g):
        start, rows = ((LOW, 24), (MIDDLE, 32))[part]
        cols = pl.ds(zs.index(way) * HALF, HALF)
        return remote(way, send.at[g, pl.ds(start - LOW, rows), cols], halo.at[g, pl.ds(start, rows), cols],
                      6 + part * 6 + zs.index(way) * 3 + g)

    def corner_copy(way, g):
        here, there = (LOW, ABOVE) if way == "xl" else (HIGH, BELOW)
        return remote(way, halo.at[g, pl.ds(here, 12)], halo.at[g, pl.ds(there, 12)],
                      18 + xs.index(way) * 3 + g)

    def start(ways, make):
        for way in ways:
            @pl.when(has[way])
            def _(way=way):
                for copy in make(way):
                    copy.start()

    def arrived(ways, make):
        for way in ways:
            @pl.when(has[back[way]])
            def _(way=way):
                for copy in make(way):
                    copy.wait_recv()

    def sent(ways, make):
        for way in ways:
            @pl.when(has[way])
            def _(way=way):
                for copy in make(way):
                    copy.wait_send()

    lower = lax.broadcasted_iota(jnp.int32, (4, 8, LANES), 1) < HALF

    def prepare(g):
        for fine, coarse, size in ((grid0, grid1, 16), (grid1, grid2, 8)):
            for r in range(size):
                pair[r, 0:2 * size] = fine[g, HALF + 2 * r] + fine[g, HALF + 2 * r + 1]
                coarse[g, HALF + r] = 0.25 * (
                    pair[r, pl.ds(0, size, stride=2)] + pair[r, pl.ds(1, size, stride=2)])
        for level, size in enumerate(SIZES):
            for n, at in enumerate(UNITS[level][1:-1]):
                rows = pl.ds(HALF + 4 * n, 4)
                first, last = grids[level][g, rows, 0:8], grids[level][g, rows, size - 8:size]
                send[g, pl.ds(at - LOW, 4)] = jnp.where(lower, first, last)

    for g in range(GROUPS):
        loads[g].wait()
    pl.semaphore_wait(barrier, sum(flag.astype(jnp.int32) for flag in has.values()))
    start(xs, lambda way: [x_copy(way, 0)])

    def ready(g, carry):
        prepare(g)
        start(zs, lambda way: [z_copy(way, 0, g)])
        return carry

    lax.fori_loop(0, GROUPS, ready, 0)
    start(xs, lambda way: [x_copy(way, level) for level in (1, 2)])
    start(zs, lambda way: [z_copy(way, 1, g) for g in range(GROUPS)])

    for load in loads[GROUPS:]:
        load.wait()
    lane = lax.broadcasted_iota(jnp.int32, (VARS, GROUPS * LANES), 1)
    row = lax.broadcasted_iota(jnp.int32, (VARS, GROUPS * LANES), 0)
    pick = jnp.where((lane >= row * LEVELS) & (lane < (row + 1) * LEVELS), 1.0, 0.0).astype(F32)
    col = lax.broadcasted_iota(jnp.int32, (8, LANES), 0)
    for level in range(GENS):
        for axis in range(2):
            raw = hk[level, :, axis]
            norm = raw / jnp.sum(raw, axis=-1, keepdims=True)
            spread = lax.dot_general(norm, pick, (((0,), (0,)), ((), ())),
                                     precision=lax.Precision.HIGHEST, preferred_element_type=F32)
            for g in range(GROUPS):
                for step in range(TAPS):
                    taps[level, axis, g, step] = jnp.broadcast_to(
                        spread[step:step + 1, g * LANES:(g + 1) * LANES], (8, LANES))
        for g in range(GROUPS):
            for j in range(1, 8):
                right = taps[level, 1, g, HALF + j] if j <= HALF else 0.0
                left = taps[level, 1, g, j - HALF] if j >= HALF else 0.0
                coef[level, g, j - 1] = jnp.where(col >= 8 - j, right, left)
    scale = jnp.dot(gw[...], pick, precision=lax.Precision.HIGHEST, preferred_element_type=F32)
    wfull[...] = jnp.zeros_like(wfull)
    for level in range(GENS):
        for g in range(GROUPS):
            wfull[0:LEVELS, 0:LEVELS] = vert[level, 2 * g]
            wfull[LEVELS:LANES, LEVELS:LANES] = vert[level, 2 * g + 1]
            whole = wfull[...] * scale[level:level + 1, g * LANES:(g + 1) * LANES]
            head = whole.astype(BF16)
            tail = (whole - head.astype(F32)).astype(BF16)
            for at in (0, LANES):
                mats[level, g, at:at + LANES, 0:LANES] = head
                mats[level, g, at:at + LANES, LANES:] = tail

    def along_x(block, level, g):
        ktaps = [taps[level, 0, g, step] for step in range(TAPS)]
        return line_sum([block[step:step + 8] for step in range(TAPS)], ktaps)

    def filters(level, g, n, wide, left):
        tiles = SIZES[level] // 8
        ktaps = [taps[level, 1, g, step] for step in range(TAPS)]
        for t in range(tiles):
            block = grids[level][g, pl.ds(8 * n, 16), 8 * t:8 * t + 8]
            wide[:, 8 + 8 * t:16 + 8 * t] = along_x(block, level, g)
        for t in range(tiles):
            first = 8 * t + HALF
            split_into(left, 64 * t, line_sum([wide[:, first + s:first + s + 8] for s in range(TAPS)], ktaps))

    def product(left, level, g):
        both = jnp.dot(left, mats[level, g], preferred_element_type=F32)
        total = both[:, 0:LANES] + both[:, LANES:]
        return total.reshape(total.shape[0] // 8, 8, LANES)

    def lanes(g):
        return pl.ds(pl.multiple_of(g * LANES, LANES), LANES)

    def put0(left, g, n):
        total = product(left[...], 0, g)
        for t in range(4):
            out[pl.ds(8 * n, 8), 8 * t:8 * t + 8, lanes(g)] = total[8 * t:8 * t + 8]

    def own0(g, n1, n2):
        filters(0, g, n1, wide0a, left0a)
        put0(left0a, g, n1)
        filters(0, g, n2, wide0b, left0b)

    def own0_all(n1, n2, after=None):
        def step(g, carry):
            put0(left0b, g - 1, n2)
            own0(g, n1, n2)
            if after is not None:
                after(g)
            return carry

        own0(0, n1, n2)
        if after is not None:
            after(0)
        lax.fori_loop(1, GROUPS, step, 0)
        put0(left0b, GROUPS - 1, n2)

    def forward(g):
        arrived(zs, lambda way: [z_copy(way, 0, g)])
        start(xs, lambda way: [corner_copy(way, g)])

    own0_all(1, 2)
    arrived(xs, lambda way: [x_copy(way, 0)])
    own0_all(0, 3, forward)
    arrived(xs, lambda way: [x_copy(way, level) for level in (1, 2)])

    def own12(g, carry):
        filters(1, g, 0, wide1a, left1a)
        filters(1, g, 1, wide1b, left1b)
        for n, left in enumerate((left1a, left1b)):
            total = product(left[...], 1, g)
            for t in range(2):
                part1[g, 8 * n:8 * n + 8, 8 * t:8 * t + 8] = total[8 * t:8 * t + 8]
        filters(2, g, 0, wide2, left2)
        part2[g] = product(left2[...], 2, g)
        return carry

    lax.fori_loop(0, GROUPS, own12, 0)

    first_row = (0, 32, 48)

    def edges(g, carry):
        arrived(zs, lambda way: [z_copy(way, 1, g)])
        arrived(xs, lambda way: [corner_copy(way, g)])
        for level in range(GENS):
            units = UNITS[level]
            for n in range(SIZES[level] // 8):
                block = jnp.concatenate([halo[g, at:at + 4] for at in units[2 * n:2 * n + 4]], axis=0)
                lines = along_x(block, level, g)
                at = first_row[level] + 8 * n
                twice[at:at + 8, 0:8] = lines
                twice[at:at + 8, 8:16] = lines
                added = line_sum([twice[at:at + 8, j:j + 8] for j in range(1, 8)],
                                 [coef[level, g, j - 1] for j in range(1, 8)])
                split_into(left_edge, 8 * at, added)

        def edge(level):
            at = 8 * first_row[level]
            return product(left_edge[at:at + 8 * SIZES[level]], level, g)

        low8 = lax.broadcasted_iota(jnp.int32, (8, 8, LANES), 1) < HALF
        total2 = part2[g] + edge(2)
        up2[:, pl.ds(0, 8, stride=2)] = total2
        up2[:, pl.ds(1, 8, stride=2)] = total2
        edge1 = edge(1)
        for n in range(2):
            mine = edge1[8 * n:8 * n + 8]
            for t in range(2):
                coarse = up2[4 * n:4 * n + 4, 8 * t:8 * t + 8]
                both = jnp.broadcast_to(coarse[:, None], (4, 2, 8, LANES)).reshape(8, 8, LANES)
                side = jnp.where(low8, mine, 0.0) if t == 0 else jnp.where(low8, 0.0, mine)
                total1 = part1[g, 8 * n:8 * n + 8, 8 * t:8 * t + 8] + side + both
                up1[8 * n:8 * n + 8, pl.ds(16 * t, 8, stride=2)] = total1
                up1[8 * n:8 * n + 8, pl.ds(16 * t + 1, 8, stride=2)] = total1
        edge0 = edge(0)
        for n in range(4):
            mine = edge0[8 * n:8 * n + 8]
            for t in range(4):
                coarse = up1[4 * n:4 * n + 4, 8 * t:8 * t + 8]
                total = jnp.broadcast_to(coarse[:, None], (4, 2, 8, LANES)).reshape(8, 8, LANES)
                if t == 0:
                    total = total + jnp.where(low8, mine, 0.0)
                if t == 3:
                    total = total + jnp.where(low8, 0.0, mine)
                out[8 * n:8 * n + 8, 8 * t:8 * t + 8, lanes(g)] += total
        return carry

    lax.fori_loop(0, GROUPS, edges, 0)

    groups = range(GROUPS)
    sent(xs, lambda way: [x_copy(way, level) for level in range(GENS)] + [corner_copy(way, g) for g in groups])
    sent(zs, lambda way: [z_copy(way, part, g) for part in range(2) for g in groups])


def solution(mesh):
    nx, ny = mesh.shape["gx"], mesh.shape["gy"]
    hbm = pltpu.MemorySpace.HBM

    def body(field, vertical, horiz_kernel, gen_weight):
        def f32(*shape):
            return pltpu.VMEM(shape, F32)

        def bf16(rows):
            return pltpu.VMEM((rows, 2 * LANES), BF16)

        operands = (field, vertical, jnp.transpose(horiz_kernel, (0, 2, 1, 3)), gen_weight)
        return pl.pallas_call(
            functools.partial(kernel, nx, ny),
            out_shape=jax.ShapeDtypeStruct(field.shape, F32),
            in_specs=[pl.BlockSpec(memory_space=hbm)] * 4,
            out_specs=pl.BlockSpec(memory_space=pltpu.MemorySpace.VMEM),
            scratch_shapes=[
                f32(GROUPS, 40, 32, LANES), f32(GROUPS, 24, 16, LANES), f32(GROUPS, 16, 8, LANES),
                f32(GROUPS, ABOVE - LOW, 8, LANES), f32(GROUPS, ROWS, 8, LANES),
                f32(8, 48, LANES), f32(8, 48, LANES), f32(8, 32, LANES), f32(8, 32, LANES), f32(8, 24, LANES),
                f32(*vertical.shape), f32(GENS, VARS, 2, TAPS), f32(*gen_weight.shape),
                f32(GENS, 2, GROUPS, TAPS, 8, LANES), f32(GENS, GROUPS, 7, 8, LANES),
                f32(LANES, LANES), pltpu.VMEM((GENS, GROUPS, 2 * LANES, 2 * LANES), BF16), f32(16, 32, LANES),
                bf16(256), bf16(256), bf16(128), bf16(128), bf16(64), f32(56, 16, LANES), bf16(448),
                f32(GROUPS, 16, 16, LANES), f32(GROUPS, 8, 8, LANES), f32(16, 32, LANES), f32(8, 16, LANES),
                pltpu.SemaphoreType.DMA((GROUPS + 3,)),
                pltpu.SemaphoreType.DMA((24,)),
                pltpu.SemaphoreType.DMA((24,)),
            ],
            compiler_params=pltpu.CompilerParams(
                collective_id=0, has_side_effects=True, vmem_limit_bytes=40 * 2 ** 20),
        )(*[pltpu.with_memory_space_constraint(operand, hbm) for operand in operands])

    return jax.shard_map(
        body, mesh=mesh, in_specs=(P("gx", "gy", None), P(), P(), P()),
        out_specs=P("gx", "gy", None), check_vma=False)
```

```python
import functools

import jax
import jax.numpy as jnp
from jax import lax
from jax.experimental import pallas as pl
from jax.experimental.pallas import tpu as pltpu
from jax.sharding import PartitionSpec as P

GENS = 3
HALF = 4
TAPS = 9
VARS = 6
LEVELS = 64
LANES = 128
GROUPS = 3
SIZES = (32, 16, 8)
MESH = pl.DeviceIdType.MESH
F32 = jnp.float32
BF16 = jnp.bfloat16

STRIP = (0, 16, 20, 22)
FIRST, SECOND = (0, 24), (24, 28)
RING = 48
BELOW, ABOVE, MIDDLE, ROWS = 0, 12, 24, 32
UNITS = (
    ((0, 0), (1, 0), (1, 24), (1, 28), (1, 32), (1, 36), (1, 40), (1, 44), (1, 12), (0, 12)),
    ((0, 4), (1, 4), (0, 24), (0, 28), (1, 16), (0, 16)),
    ((0, 8), (1, 8), (1, 20), (0, 20)),
)


def line_sum(pieces, taps):
    total = taps[0] * pieces[0]
    for piece, tap in zip(pieces[1:], taps[1:]):
        total = total + tap * piece
    return total


def split_into(ref, at, values):
    rows = values.shape[0] * values.shape[1]
    flat = values.reshape(rows, LANES)
    head = flat.astype(BF16)
    ref[at:at + rows, 0:LANES] = head
    ref[at:at + rows, LANES:] = (flat - head.astype(F32)).astype(BF16)


def kernel(nx, ny, field, vertical, horiz, weight, out,
           grid0, grid1, grid2, x_out, x_in, z_out, z_in, halo,
           wide0a, wide0b, wide0c, wide1a, wide2, strip1, strip2,
           vert, hk, gw, scale, taps, coef, wfull, mats, pair, quad,
           left0a, left0b, left0c, left1a, left2, twice, left_edge, part1, part2, up1, up2,
           load_sem, send_sem, recv_sem, corner_ready):
    gx, gy = lax.axis_index("gx"), lax.axis_index("gy")
    grids = (grid0, grid1, grid2)

    has = {"xl": gx > 0, "xr": gx < nx - 1, "zl": gy > 0, "zr": gy < ny - 1}
    ids = {"xl": {"gx": gx - 1}, "xr": {"gx": gx + 1}, "zl": {"gy": gy - 1}, "zr": {"gy": gy + 1}}
    back = {"xl": "xr", "xr": "xl", "zl": "zr", "zr": "zl"}
    xs, zs = ("xl", "xr"), ("zl", "zr")

    first = (gx == 0) & (gy == 0)
    near = {"xl": (gx == 1) & (gy == 0), "zl": (gx == 0) & (gy == 1)}
    now = {way: has[way] & jnp.logical_not(near[way]) if way in near else has[way] for way in has}

    barrier = pltpu.get_barrier_semaphore()
    for way in has:
        @pl.when(has[way] & jnp.logical_not(first))
        def _(way=way):
            pl.semaphore_signal(barrier, inc=1, device_id=ids[way], device_id_type=MESH)

    @pl.when(first)
    def _():
        pl.semaphore_wait(barrier, 2)
        for way in ("xr", "zr"):
            pl.semaphore_signal(corner_ready, inc=1, device_id=ids[way], device_id_type=MESH)

    small = [
        pltpu.make_async_copy(src, dst, load_sem.at[GROUPS + n])
        for n, (src, dst) in enumerate(((horiz, hk), (weight, gw), (vertical, vert)))
    ]
    loads = [
        pltpu.make_async_copy(field.at[:, :, pl.ds(g * LANES, LANES)], grid0.at[g], load_sem.at[g])
        for g in range(GROUPS)
    ]
    for load in small[:2] + loads + small[2:]:
        load.start()

    for way in has:
        @pl.when(jnp.logical_not(has[way]))
        def _(way=way):
            if way in xs:
                x_in[xs.index(way)] = jnp.zeros((GROUPS, STRIP[3], 8, LANES), F32)
                at = BELOW if way == "xl" else ABOVE
                halo[:, at:at + 12] = jnp.zeros((GROUPS, 12, 8, LANES), F32)
            else:
                at = HALF if way == "zl" else 0
                z_in[:, :, at:at + HALF] = jnp.zeros((GROUPS, 52, HALF, LANES), F32)
    for wide, size in ((wide0a, 32), (wide0b, 32), (wide0c, 32), (wide1a, 16), (wide2, 8)):
        wide[:, 0:8] = jnp.zeros((8, 8, LANES), F32)
        wide[:, size + 8:] = jnp.zeros((8, 8, LANES), F32)

    def remote(way, src, dst, slot):
        return pltpu.make_async_remote_copy(
            src_ref=src, dst_ref=dst, send_sem=send_sem.at[slot], recv_sem=recv_sem.at[slot],
            device_id=ids[way], device_id_type=MESH)

    def x_copy(way, g):
        n = xs.index(way)
        return remote(way, x_out.at[n, g], x_in.at[1 - n, g], n * 3 + g)

    def z_copy(way, part, g):
        start, rows = (FIRST, SECOND)[part]
        cols = pl.ds(zs.index(way) * HALF, HALF)
        return remote(way, z_out.at[g, pl.ds(start, rows), cols], z_in.at[g, pl.ds(start, rows), cols],
                      6 + part * 6 + zs.index(way) * 3 + g)

    def corner_copy(way, g):
        here, there = (0, ABOVE) if way == "xl" else (12, BELOW)
        return remote(way, z_in.at[g, pl.ds(here, 12)], halo.at[g, pl.ds(there, 12)],
                      18 + xs.index(way) * 3 + g)

    def start(ways, make, gate=has):
        for way in ways:
            @pl.when(gate[way])
            def _(way=way):
                for copy in make(way):
                    copy.start()

    def arrived(ways, make):
        for way in ways:
            @pl.when(has[back[way]])
            def _(way=way):
                for copy in make(way):
                    copy.wait_recv()

    def sent(ways, make):
        for way in ways:
            @pl.when(has[way])
            def _(way=way):
                for copy in make(way):
                    copy.wait_send()

    lower = lax.broadcasted_iota(jnp.int32, (4, 8, LANES), 1) < HALF

    def prepare(g, carry):
        for fine, coarse, size in ((grid0, grid1, 16), (grid1, grid2, 8)):
            for r in range(size):
                pair[r, 0:2 * size] = fine[g, 2 * r] + fine[g, 2 * r + 1]
                coarse[g, r] = 0.25 * (
                    pair[r, pl.ds(0, size, stride=2)] + pair[r, pl.ds(1, size, stride=2)])
        for level, size in enumerate(SIZES):
            rows = ((0, 4), (size - 4, size)) if level == 0 else ((2, 4), (size - 4, size - 2))
            for n, (low, high) in enumerate(rows):
                x_out[n, g, STRIP[level]:STRIP[level + 1]] = grids[level][g, low:high].reshape(-1, 8, LANES)
        for level, here, there in (
                (0, 0, 0), (1, 0, 4), (2, 0, 8), (0, 28, 12), (1, 12, 16), (2, 4, 20),
                (0, 4, 24), (0, 8, 28), (0, 12, 32), (0, 16, 36), (0, 20, 40), (0, 24, 44)):
            size, rows = SIZES[level], pl.ds(here, 4)
            head, tail = grids[level][g, rows, 0:8], grids[level][g, rows, size - 8:size]
            z_out[g, there:there + 4] = jnp.where(lower, head, tail)
        for k in range(4):
            for odd in range(2):
                z_out[g, RING + k, 2 * odd:2 * odd + 2] = grid1[g, 4 + 2 * k + odd, 2:4]
                z_out[g, RING + k, 4 + 2 * odd:6 + 2 * odd] = grid1[g, 4 + 2 * k + odd, 12:14]
        return carry

    small[0].wait()
    small[1].wait()
    lane = lax.broadcasted_iota(jnp.int32, (VARS, GROUPS * LANES), 1)
    row = lax.broadcasted_iota(jnp.int32, (VARS, GROUPS * LANES), 0)
    pick = jnp.where((lane >= row * LEVELS) & (lane < (row + 1) * LEVELS), 1.0, 0.0).astype(F32)
    col = lax.broadcasted_iota(jnp.int32, (8, LANES), 0)
    for level in range(GENS):
        for axis in range(2):
            raw = hk[level, :, axis]
            norm = raw / jnp.sum(raw, axis=-1, keepdims=True)
            spread = lax.dot_general(norm, pick, (((0,), (0,)), ((), ())),
                                     precision=lax.Precision.HIGHEST, preferred_element_type=F32)
            for g in range(GROUPS):
                for step in range(TAPS):
                    taps[level, axis, g, step] = jnp.broadcast_to(
                        spread[step:step + 1, g * LANES:(g + 1) * LANES], (8, LANES))
        for g in range(GROUPS):
            for j in range(1, 8):
                right = taps[level, 1, g, HALF + j] if j <= HALF else 0.0
                left = taps[level, 1, g, j - HALF] if j >= HALF else 0.0
                coef[level, g, j - 1] = jnp.where(col >= 8 - j, right, left)
    scale[...] = jnp.dot(gw[...], pick, precision=lax.Precision.HIGHEST, preferred_element_type=F32)

    def matrices():
        small[2].wait()
        wfull[...] = jnp.zeros_like(wfull)
        for level in range(GENS):
            for g in range(GROUPS):
                wfull[0:LEVELS, 0:LEVELS] = vert[level, 2 * g]
                wfull[LEVELS:LANES, LEVELS:LANES] = vert[level, 2 * g + 1]
                whole = wfull[...] * scale[level:level + 1, g * LANES:(g + 1) * LANES]
                head = whole.astype(BF16)
                tail = (whole - head.astype(F32)).astype(BF16)
                for at in (0, LANES):
                    mats[level, g, at:at + LANES, 0:LANES] = head
                    mats[level, g, at:at + LANES, LANES:] = tail

    for g in range(GROUPS):
        loads[g].wait()
    lax.fori_loop(0, GROUPS, prepare, 0)
    pl.when(jnp.logical_not(first))(matrices)

    @pl.when(jnp.logical_not(first))
    def _():
        pl.semaphore_wait(barrier, sum(flag.astype(jnp.int32) for flag in now.values()))

    for g in range(GROUPS):
        start(zs, lambda way: [z_copy(way, 0, g)], now)
        start(xs, lambda way: [x_copy(way, g)], now)
    start(zs, lambda way: [z_copy(way, 1, g) for g in range(GROUPS)], now)
    pl.when(first)(matrices)

    def along_x(block, level, g):
        ktaps = [taps[level, 0, g, step] for step in range(TAPS)]
        count = block.shape[0] - 2 * HALF
        return line_sum([block[step:step + count] for step in range(TAPS)], ktaps)

    def along_y(level, g, wide, left):
        ktaps = [taps[level, 1, g, step] for step in range(TAPS)]
        for t in range(SIZES[level] // 8):
            at = 8 * t + HALF
            split_into(left, 64 * t, line_sum([wide[:, at + s:at + s + 8] for s in range(TAPS)], ktaps))

    def strips(g):
        for side in range(2):
            for level, fine, size in ((1, x_in, 16), (2, strip1, 8)):
                strip, tiles = (strip1, strip2)[level - 1], size // 8
                for r in range(2):
                    own, ring = (2 + r, r) if side == 0 else (r, 2 + r)
                    for t in range(2 * tiles):
                        if level == 1:
                            both = x_in[side, g, 8 * r + t] + x_in[side, g, 8 * r + 4 + t]
                        else:
                            both = strip1[side, 2 * r, 8 * t:8 * t + 8] + strip1[side, 2 * r + 1, 8 * t:8 * t + 8]
                        pair[2 * side + r, 8 * t:8 * t + 8] = both
                    strip[side, own] = 0.25 * (
                        pair[2 * side + r, pl.ds(0, size, stride=2)] + pair[2 * side + r, pl.ds(1, size, stride=2)])
                    for t in range(tiles):
                        strip[side, ring, 8 * t:8 * t + 8] = x_in[side, g, STRIP[level] + r * tiles + t]

    def strip(side, level, g, t):
        if level == 0:
            return jnp.concatenate([x_in[side, g, pl.ds(4 * r + t, 1)] for r in range(HALF)], axis=0)
        return (strip1, strip2)[level - 1][side, :, 8 * t:8 * t + 8]

    def inner_rows(level, g, row, wide, left):
        for t in range(SIZES[level] // 8):
            wide[:, 8 + 8 * t:16 + 8 * t] = along_x(
                grids[level][g, row - HALF:row + 12, 8 * t:8 * t + 8], level, g)
        along_y(level, g, wide, left)

    def outer_rows(level, g, wide, left):
        size = SIZES[level]
        for t in range(size // 8):
            cols, to = slice(8 * t, 8 * t + 8), slice(8 + 8 * t, 16 + 8 * t)
            low, high = strip(0, level, g, t), strip(1, level, g, t)
            if level == 2:
                wide[:, to] = along_x(jnp.concatenate([low, grid2[g], high], axis=0), level, g)
            else:
                wide[0:4, to] = along_x(jnp.concatenate([low, grids[level][g, 0:8, cols]], axis=0), level, g)
                wide[4:8, to] = along_x(
                    jnp.concatenate([grids[level][g, size - 8:size, cols], high], axis=0), level, g)
        along_y(level, g, wide, left)

    def product(left, level, g):
        both = jnp.dot(left, mats[level, g], preferred_element_type=F32)
        total = both[:, 0:LANES] + both[:, LANES:]
        return total.reshape(total.shape[0] // 8, 8, LANES)

    def lanes(g):
        return pl.ds(pl.multiple_of(g * LANES, LANES), LANES)

    def put0(left, g, low, high):
        total = product(left[...], 0, g)
        for t in range(4):
            out[low:low + 4, 8 * t:8 * t + 8, lanes(g)] = total[8 * t:8 * t + 4]
            out[high:high + 4, 8 * t:8 * t + 8, lanes(g)] = total[8 * t + 4:8 * t + 8]

    def put1(left, g, low, high):
        total = product(left[...], 1, g)
        for t in range(2):
            part1[g, low:low + 4, 8 * t:8 * t + 8] = total[8 * t:8 * t + 4]
            part1[g, high:high + 4, 8 * t:8 * t + 8] = total[8 * t + 4:8 * t + 8]

    def inner_four(g):
        inner_rows(0, g, 4, wide0a, left0a)
        put0(left0a, g, 4, 8)
        inner_rows(0, g, 12, wide0b, left0b)
        put0(left0b, g, 12, 16)
        inner_rows(1, g, 4, wide1a, left1a)
        put1(left1a, g, 4, 8)
        inner_rows(0, g, 20, wide0c, left0c)

    def inner(g, carry):
        put0(left0c, g - 1, 20, 24)
        inner_four(g)
        return carry

    inner_four(0)
    lax.fori_loop(1, GROUPS, inner, 0)
    put0(left0c, GROUPS - 1, 20, 24)

    for way in near:
        @pl.when(near[way])
        def _(way=way):
            pl.semaphore_wait(corner_ready, 1)
            if way == "xl":
                copies = [x_copy(way, g) for g in range(GROUPS)]
            else:
                copies = [z_copy(way, part, g) for part in range(2) for g in range(GROUPS)]
            for copy in copies:
                copy.start()

    def derive(g):
        for k in range(2):
            rows = z_in[g, 28 + 8 * k:36 + 8 * k].reshape(4, 2, 8, LANES)
            quad[k] = (rows[:, 0] + rows[:, 1]).reshape(32, LANES)
            means = 0.25 * (quad[k, pl.ds(0, 16, stride=2)] + quad[k, pl.ds(1, 16, stride=2)])
            for r in range(4):
                at, ring, odd = MIDDLE + 4 * k + r, RING + 2 * k + r // 2, r % 2
                halo[g, at, 0:2] = means[4 * r:4 * r + 2]
                halo[g, at, 6:8] = means[4 * r + 2:4 * r + 4]
                halo[g, at, 2:4] = z_in[g, ring, 2 * odd:2 * odd + 2]
                halo[g, at, 4:6] = z_in[g, ring, 4 + 2 * odd:6 + 2 * odd]

    def forward(g):
        arrived(zs, lambda way: [z_copy(way, 0, g)])
        start(xs, lambda way: [corner_copy(way, g)])

    def forward_first(g, carry):
        forward(g)
        return carry

    @pl.when(first)
    def _():
        lax.fori_loop(0, GROUPS, forward_first, 0)

    def outer(g, carry):
        @pl.when(jnp.logical_not(first))
        def _():
            forward(g)

        arrived(xs, lambda way: [x_copy(way, g)])
        strips(g)
        outer_rows(0, g, wide0a, left0a)
        put0(left0a, g, 0, 28)
        outer_rows(1, g, wide1a, left1a)
        put1(left1a, g, 0, 12)
        outer_rows(2, g, wide2, left2)
        part2[g] = product(left2[...], 2, g)
        return carry

    lax.fori_loop(0, GROUPS, outer, 0)

    groups = range(GROUPS)
    sent(xs, lambda way: [x_copy(way, g) for g in groups] + [corner_copy(way, g) for g in groups])
    sent(zs, lambda way: [z_copy(way, part, g) for part in range(2) for g in groups])

    first_row = (0, 32, 48)

    def edge_lines(level, g, n):
        block = jnp.concatenate(
            [(z_in if near_z else halo)[g, at:at + 4] for near_z, at in UNITS[level][2 * n:2 * n + 4]], axis=0)
        lines = along_x(block, level, g)
        at = first_row[level] + 8 * n
        twice[at:at + 8, 0:8] = lines
        twice[at:at + 8, 8:16] = lines
        added = line_sum([twice[at:at + 8, j:j + 8] for j in range(1, 8)],
                         [coef[level, g, j - 1] for j in range(1, 8)])
        split_into(left_edge, 8 * at, added)

    def edge(level, g):
        at = 8 * first_row[level]
        return product(left_edge[at:at + 8 * SIZES[level]], level, g)

    low8 = lax.broadcasted_iota(jnp.int32, (8, 8, LANES), 1) < HALF

    def edges(g, carry):
        arrived(zs, lambda way: [z_copy(way, 1, g)])
        edge_lines(0, g, 1)
        edge_lines(0, g, 2)
        derive(g)
        arrived(xs, lambda way: [corner_copy(way, g)])
        edge_lines(2, g, 0)
        total2 = part2[g] + edge(2, g)
        up2[:, pl.ds(0, 8, stride=2)] = total2
        up2[:, pl.ds(1, 8, stride=2)] = total2
        edge_lines(1, g, 0)
        edge_lines(1, g, 1)
        edge1 = edge(1, g)
        for n in range(2):
            mine = edge1[8 * n:8 * n + 8]
            for t in range(2):
                coarse = up2[4 * n:4 * n + 4, 8 * t:8 * t + 8]
                both = jnp.broadcast_to(coarse[:, None], (4, 2, 8, LANES)).reshape(8, 8, LANES)
                side = jnp.where(low8, mine, 0.0) if t == 0 else jnp.where(low8, 0.0, mine)
                total1 = part1[g, 8 * n:8 * n + 8, 8 * t:8 * t + 8] + side + both
                up1[8 * n:8 * n + 8, pl.ds(16 * t, 8, stride=2)] = total1
                up1[8 * n:8 * n + 8, pl.ds(16 * t + 1, 8, stride=2)] = total1
        edge_lines(0, g, 0)
        edge_lines(0, g, 3)
        edge0 = edge(0, g)
        for n in range(4):
            mine = edge0[8 * n:8 * n + 8]
            for t in range(4):
                coarse = up1[4 * n:4 * n + 4, 8 * t:8 * t + 8]
                total = jnp.broadcast_to(coarse[:, None], (4, 2, 8, LANES)).reshape(8, 8, LANES)
                if t == 0:
                    total = total + jnp.where(low8, mine, 0.0)
                if t == 3:
                    total = total + jnp.where(low8, 0.0, mine)
                out[8 * n:8 * n + 8, 8 * t:8 * t + 8, lanes(g)] += total
        return carry

    lax.fori_loop(0, GROUPS, edges, 0)


def solution(mesh):
    nx, ny = mesh.shape["gx"], mesh.shape["gy"]
    hbm = pltpu.MemorySpace.HBM

    def body(field, vertical, horiz_kernel, gen_weight):
        def f32(*shape):
            return pltpu.VMEM(shape, F32)

        def bf16(rows):
            return pltpu.VMEM((rows, 2 * LANES), BF16)

        operands = (field, vertical, jnp.transpose(horiz_kernel, (0, 2, 1, 3)), gen_weight)
        return pl.pallas_call(
            functools.partial(kernel, nx, ny),
            out_shape=jax.ShapeDtypeStruct(field.shape, F32),
            in_specs=[pl.BlockSpec(memory_space=hbm)] * 4,
            out_specs=pl.BlockSpec(memory_space=pltpu.MemorySpace.VMEM),
            scratch_shapes=[
                f32(GROUPS, 32, 32, LANES), f32(GROUPS, 16, 16, LANES), f32(GROUPS, 8, 8, LANES),
                f32(2, GROUPS, STRIP[3], 8, LANES), f32(2, GROUPS, STRIP[3], 8, LANES),
                f32(GROUPS, 52, 8, LANES), f32(GROUPS, 52, 8, LANES), f32(GROUPS, ROWS, 8, LANES),
                f32(8, 48, LANES), f32(8, 48, LANES), f32(8, 48, LANES),
                f32(8, 32, LANES), f32(8, 24, LANES), f32(2, 4, 16, LANES), f32(2, 4, 8, LANES),
                f32(*vertical.shape), f32(GENS, VARS, 2, TAPS), f32(*gen_weight.shape),
                f32(GENS, GROUPS * LANES),
                f32(GENS, 2, GROUPS, TAPS, 8, LANES), f32(GENS, GROUPS, 7, 8, LANES),
                f32(LANES, LANES), pltpu.VMEM((GENS, GROUPS, 2 * LANES, 2 * LANES), BF16),
                f32(16, 32, LANES), f32(2, 32, LANES),
                bf16(256), bf16(256), bf16(256), bf16(128), bf16(64), f32(56, 16, LANES), bf16(448),
                f32(GROUPS, 16, 16, LANES), f32(GROUPS, 8, 8, LANES), f32(16, 32, LANES), f32(8, 16, LANES),
                pltpu.SemaphoreType.DMA((GROUPS + 3,)),
                pltpu.SemaphoreType.DMA((24,)),
                pltpu.SemaphoreType.DMA((24,)),
                pltpu.SemaphoreType.REGULAR,
            ],
            compiler_params=pltpu.CompilerParams(
                collective_id=0, has_side_effects=True, vmem_limit_bytes=40 * 2 ** 20),
        )(*[pltpu.with_memory_space_constraint(operand, hbm) for operand in operands])

    return jax.shard_map(
        body, mesh=mesh, in_specs=(P("gx", "gy", None), P(), P(), P()),
        out_specs=P("gx", "gy", None), check_vma=False)
```

```python
import functools

import jax
import jax.numpy as jnp
from jax import lax
from jax.experimental import pallas as pl
from jax.experimental.pallas import tpu as pltpu
from jax.sharding import PartitionSpec as P

GENS = 3
HALF = 4
TAPS = 9
VARS = 6
LEVELS = 64
LANES = 128
GROUPS = 3
SIZES = (32, 16, 8)
MESH = pl.DeviceIdType.MESH
F32 = jnp.float32
BF16 = jnp.bfloat16

STRIP = (0, 16, 20, 22)
FIRST, SECOND = (0, 24), (24, 28)
RING = 48
BELOW, ABOVE, MIDDLE, ROWS = 0, 12, 24, 32
UNITS = (
    ((0, 0), (1, 0), (1, 24), (1, 28), (1, 32), (1, 36), (1, 40), (1, 44), (1, 12), (0, 12)),
    ((0, 4), (1, 4), (0, 24), (0, 28), (1, 16), (0, 16)),
    ((0, 8), (1, 8), (1, 20), (0, 20)),
)


def line_sum(pieces, taps):
    total = taps[0] * pieces[0]
    for piece, tap in zip(pieces[1:], taps[1:]):
        total = total + tap * piece
    return total


def split_into(ref, at, values):
    rows = values.shape[0] * values.shape[1]
    flat = values.reshape(rows, LANES)
    head = flat.astype(BF16)
    ref[at:at + rows, 0:LANES] = head
    ref[at:at + rows, LANES:] = (flat - head.astype(F32)).astype(BF16)


def kernel(nx, ny, field, vertical, horiz, weight, out,
           grid0, grid1, grid2, x_out, x_in, z_out, z_in, halo,
           wide0a, wide0b, wide0c, wide1a, wide2, strip1, strip2,
           vert, hk, gw, scale, taps, coef, wfull, mats, pair, quad,
           left0a, left0b, left0c, left1a, left2, twice, left_edge, part1, part2, up1, up2,
           load_sem, send_sem, recv_sem, corner_ready):
    gx, gy = lax.axis_index("gx"), lax.axis_index("gy")
    grids = (grid0, grid1, grid2)

    has = {"xl": gx > 0, "xr": gx < nx - 1, "zl": gy > 0, "zr": gy < ny - 1}
    ids = {"xl": {"gx": gx - 1}, "xr": {"gx": gx + 1}, "zl": {"gy": gy - 1}, "zr": {"gy": gy + 1}}
    back = {"xl": "xr", "xr": "xl", "zl": "zr", "zr": "zl"}
    xs, zs = ("xl", "xr"), ("zl", "zr")

    first = (gx == 0) & (gy == 0)
    near = {"xl": (gx == 1) & (gy == 0), "zl": (gx == 0) & (gy == 1)}
    now = {way: has[way] & jnp.logical_not(near[way]) if way in near else has[way] for way in has}

    barrier = pltpu.get_barrier_semaphore()
    for way in has:
        @pl.when(has[way] & jnp.logical_not(first))
        def _(way=way):
            pl.semaphore_signal(barrier, inc=1, device_id=ids[way], device_id_type=MESH)

    @pl.when(first)
    def _():
        pl.semaphore_wait(barrier, 2)
        for way in ("xr", "zr"):
            pl.semaphore_signal(corner_ready, inc=1, device_id=ids[way], device_id_type=MESH)

    small = [
        pltpu.make_async_copy(src, dst, load_sem.at[GROUPS + n])
        for n, (src, dst) in enumerate(((horiz, hk), (weight, gw), (vertical, vert)))
    ]
    loads = [
        pltpu.make_async_copy(field.at[:, :, pl.ds(g * LANES, LANES)], grid0.at[g], load_sem.at[g])
        for g in range(GROUPS)
    ]
    for load in small[:2] + loads + small[2:]:
        load.start()

    for way in has:
        @pl.when(jnp.logical_not(has[way]))
        def _(way=way):
            if way in xs:
                x_in[xs.index(way)] = jnp.zeros((GROUPS, STRIP[3], 8, LANES), F32)
                at = BELOW if way == "xl" else ABOVE
                halo[:, at:at + 12] = jnp.zeros((GROUPS, 12, 8, LANES), F32)
            else:
                at = HALF if way == "zl" else 0
                z_in[:, :, at:at + HALF] = jnp.zeros((GROUPS, 52, HALF, LANES), F32)
    for wide, size in ((wide0a, 32), (wide0b, 32), (wide0c, 32), (wide1a, 16), (wide2, 8)):
        wide[:, 0:8] = jnp.zeros((8, 8, LANES), F32)
        wide[:, size + 8:] = jnp.zeros((8, 8, LANES), F32)

    def remote(way, src, dst, slot):
        return pltpu.make_async_remote_copy(
            src_ref=src, dst_ref=dst, send_sem=send_sem.at[slot], recv_sem=recv_sem.at[slot],
            device_id=ids[way], device_id_type=MESH)

    def x_copy(way, g):
        n = xs.index(way)
        return remote(way, x_out.at[n, g], x_in.at[1 - n, g], n * 3 + g)

    def z_copy(way, part, g):
        start, rows = (FIRST, SECOND)[part]
        cols = pl.ds(zs.index(way) * HALF, HALF)
        return remote(way, z_out.at[g, pl.ds(start, rows), cols], z_in.at[g, pl.ds(start, rows), cols],
                      6 + part * 6 + zs.index(way) * 3 + g)

    def corner_copy(way, g):
        here, there = (0, ABOVE) if way == "xl" else (12, BELOW)
        return remote(way, z_in.at[g, pl.ds(here, 12)], halo.at[g, pl.ds(there, 12)],
                      18 + xs.index(way) * 3 + g)

    def start(ways, make, gate=has):
        for way in ways:
            @pl.when(gate[way])
            def _(way=way):
                for copy in make(way):
                    copy.start()

    def arrived(ways, make):
        for way in ways:
            @pl.when(has[back[way]])
            def _(way=way):
                for copy in make(way):
                    copy.wait_recv()

    def sent(ways, make):
        for way in ways:
            @pl.when(has[way])
            def _(way=way):
                for copy in make(way):
                    copy.wait_send()

    lower = lax.broadcasted_iota(jnp.int32, (4, 8, LANES), 1) < HALF

    def prepare(g, carry):
        for fine, coarse, size in ((grid0, grid1, 16), (grid1, grid2, 8)):
            for r in range(size):
                pair[r, 0:2 * size] = fine[g, 2 * r] + fine[g, 2 * r + 1]
                coarse[g, r] = 0.25 * (
                    pair[r, pl.ds(0, size, stride=2)] + pair[r, pl.ds(1, size, stride=2)])
        for level, size in enumerate(SIZES):
            rows = ((0, 4), (size - 4, size)) if level == 0 else ((2, 4), (size - 4, size - 2))
            for n, (low, high) in enumerate(rows):
                x_out[n, g, STRIP[level]:STRIP[level + 1]] = grids[level][g, low:high].reshape(-1, 8, LANES)
        for level, here, there in (
                (0, 0, 0), (1, 0, 4), (2, 0, 8), (0, 28, 12), (1, 12, 16), (2, 4, 20),
                (0, 4, 24), (0, 8, 28), (0, 12, 32), (0, 16, 36), (0, 20, 40), (0, 24, 44)):
            size, rows = SIZES[level], pl.ds(here, 4)
            head, tail = grids[level][g, rows, 0:8], grids[level][g, rows, size - 8:size]
            z_out[g, there:there + 4] = jnp.where(lower, head, tail)
        for k in range(4):
            for odd in range(2):
                z_out[g, RING + k, 2 * odd:2 * odd + 2] = grid1[g, 4 + 2 * k + odd, 2:4]
                z_out[g, RING + k, 4 + 2 * odd:6 + 2 * odd] = grid1[g, 4 + 2 * k + odd, 12:14]
        return carry

    small[0].wait()
    small[1].wait()
    lane = lax.broadcasted_iota(jnp.int32, (VARS, GROUPS * LANES), 1)
    row = lax.broadcasted_iota(jnp.int32, (VARS, GROUPS * LANES), 0)
    pick = jnp.where((lane >= row * LEVELS) & (lane < (row + 1) * LEVELS), 1.0, 0.0).astype(F32)
    col = lax.broadcasted_iota(jnp.int32, (8, LANES), 0)
    for level in range(GENS):
        for axis in range(2):
            raw = hk[level, :, axis]
            norm = raw / jnp.sum(raw, axis=-1, keepdims=True)
            spread = lax.dot_general(norm, pick, (((0,), (0,)), ((), ())),
                                     precision=lax.Precision.HIGHEST, preferred_element_type=F32)
            for g in range(GROUPS):
                for step in range(TAPS):
                    taps[level, axis, g, step] = jnp.broadcast_to(
                        spread[step:step + 1, g * LANES:(g + 1) * LANES], (8, LANES))
        for g in range(GROUPS):
            for j in range(1, 8):
                right = taps[level, 1, g, HALF + j] if j <= HALF else 0.0
                left = taps[level, 1, g, j - HALF] if j >= HALF else 0.0
                coef[level, g, j - 1] = jnp.where(col >= 8 - j, right, left)
    scale[...] = jnp.dot(gw[...], pick, precision=lax.Precision.HIGHEST, preferred_element_type=F32)

    def matrices():
        small[2].wait()
        wfull[...] = jnp.zeros_like(wfull)
        for level in range(GENS):
            for g in range(GROUPS):
                wfull[0:LEVELS, 0:LEVELS] = vert[level, 2 * g]
                wfull[LEVELS:LANES, LEVELS:LANES] = vert[level, 2 * g + 1]
                whole = wfull[...] * scale[level:level + 1, g * LANES:(g + 1) * LANES]
                head = whole.astype(BF16)
                tail = (whole - head.astype(F32)).astype(BF16)
                for at in (0, LANES):
                    mats[level, g, at:at + LANES, 0:LANES] = head
                    mats[level, g, at:at + LANES, LANES:] = tail

    for g in range(GROUPS):
        loads[g].wait()
    lax.fori_loop(0, GROUPS, prepare, 0)

    @pl.when(jnp.logical_not(first))
    def _():
        pl.semaphore_wait(barrier, sum(flag.astype(jnp.int32) for flag in now.values()))

    start(zs, lambda way: [z_copy(way, 0, g) for g in range(GROUPS)], now)
    start(xs, lambda way: [x_copy(way, g) for g in range(GROUPS)], now)
    start(zs, lambda way: [z_copy(way, 1, g) for g in range(GROUPS)], now)
    matrices()

    def along_x(block, level, g):
        ktaps = [taps[level, 0, g, step] for step in range(TAPS)]
        count = block.shape[0] - 2 * HALF
        return line_sum([block[step:step + count] for step in range(TAPS)], ktaps)

    def along_y(level, g, wide, left):
        ktaps = [taps[level, 1, g, step] for step in range(TAPS)]
        for t in range(SIZES[level] // 8):
            at = 8 * t + HALF
            split_into(left, 64 * t, line_sum([wide[:, at + s:at + s + 8] for s in range(TAPS)], ktaps))

    def strips(g):
        for side in range(2):
            for level, fine, size in ((1, x_in, 16), (2, strip1, 8)):
                strip, tiles = (strip1, strip2)[level - 1], size // 8
                for r in range(2):
                    own, ring = (2 + r, r) if side == 0 else (r, 2 + r)
                    for t in range(2 * tiles):
                        if level == 1:
                            both = x_in[side, g, 8 * r + t] + x_in[side, g, 8 * r + 4 + t]
                        else:
                            both = strip1[side, 2 * r, 8 * t:8 * t + 8] + strip1[side, 2 * r + 1, 8 * t:8 * t + 8]
                        pair[2 * side + r, 8 * t:8 * t + 8] = both
                    strip[side, own] = 0.25 * (
                        pair[2 * side + r, pl.ds(0, size, stride=2)] + pair[2 * side + r, pl.ds(1, size, stride=2)])
                    for t in range(tiles):
                        strip[side, ring, 8 * t:8 * t + 8] = x_in[side, g, STRIP[level] + r * tiles + t]

    def strip(side, level, g, t):
        if level == 0:
            return jnp.concatenate([x_in[side, g, pl.ds(4 * r + t, 1)] for r in range(HALF)], axis=0)
        return (strip1, strip2)[level - 1][side, :, 8 * t:8 * t + 8]

    def inner_rows(level, g, row, wide, left):
        for t in range(SIZES[level] // 8):
            wide[:, 8 + 8 * t:16 + 8 * t] = along_x(
                grids[level][g, row - HALF:row + 12, 8 * t:8 * t + 8], level, g)
        along_y(level, g, wide, left)

    def outer_rows(level, g, wide, left):
        size = SIZES[level]
        for t in range(size // 8):
            cols, to = slice(8 * t, 8 * t + 8), slice(8 + 8 * t, 16 + 8 * t)
            low, high = strip(0, level, g, t), strip(1, level, g, t)
            if level == 2:
                wide[:, to] = along_x(jnp.concatenate([low, grid2[g], high], axis=0), level, g)
            else:
                wide[0:4, to] = along_x(jnp.concatenate([low, grids[level][g, 0:8, cols]], axis=0), level, g)
                wide[4:8, to] = along_x(
                    jnp.concatenate([grids[level][g, size - 8:size, cols], high], axis=0), level, g)
        along_y(level, g, wide, left)

    def product(left, level, g):
        both = jnp.dot(left, mats[level, g], preferred_element_type=F32)
        total = both[:, 0:LANES] + both[:, LANES:]
        return total.reshape(total.shape[0] // 8, 8, LANES)

    def lanes(g):
        return pl.ds(pl.multiple_of(g * LANES, LANES), LANES)

    def put0(left, g, low, high):
        total = product(left[...], 0, g)
        for t in range(4):
            out[low:low + 4, 8 * t:8 * t + 8, lanes(g)] = total[8 * t:8 * t + 4]
            out[high:high + 4, 8 * t:8 * t + 8, lanes(g)] = total[8 * t + 4:8 * t + 8]

    def put1(left, g, low, high):
        total = product(left[...], 1, g)
        for t in range(2):
            part1[g, low:low + 4, 8 * t:8 * t + 8] = total[8 * t:8 * t + 4]
            part1[g, high:high + 4, 8 * t:8 * t + 8] = total[8 * t + 4:8 * t + 8]

    def inner_four(g):
        inner_rows(0, g, 4, wide0a, left0a)
        put0(left0a, g, 4, 8)
        inner_rows(0, g, 12, wide0b, left0b)
        put0(left0b, g, 12, 16)
        inner_rows(1, g, 4, wide1a, left1a)
        put1(left1a, g, 4, 8)
        inner_rows(0, g, 20, wide0c, left0c)

    def inner(g, carry):
        put0(left0c, g - 1, 20, 24)
        inner_four(g)
        return carry

    inner_four(0)
    lax.fori_loop(1, GROUPS, inner, 0)
    put0(left0c, GROUPS - 1, 20, 24)

    for way in near:
        @pl.when(near[way])
        def _(way=way):
            pl.semaphore_wait(corner_ready, 1)
            if way == "xl":
                copies = [x_copy(way, g) for g in range(GROUPS)]
            else:
                copies = [z_copy(way, part, g) for part in range(2) for g in range(GROUPS)]
            for copy in copies:
                copy.start()

    def derive(g):
        for k in range(2):
            rows = z_in[g, 28 + 8 * k:36 + 8 * k].reshape(4, 2, 8, LANES)
            quad[k] = (rows[:, 0] + rows[:, 1]).reshape(32, LANES)
            means = 0.25 * (quad[k, pl.ds(0, 16, stride=2)] + quad[k, pl.ds(1, 16, stride=2)])
            for r in range(4):
                at, ring, odd = MIDDLE + 4 * k + r, RING + 2 * k + r // 2, r % 2
                halo[g, at, 0:2] = means[4 * r:4 * r + 2]
                halo[g, at, 6:8] = means[4 * r + 2:4 * r + 4]
                halo[g, at, 2:4] = z_in[g, ring, 2 * odd:2 * odd + 2]
                halo[g, at, 4:6] = z_in[g, ring, 4 + 2 * odd:6 + 2 * odd]

    def forward(g):
        arrived(zs, lambda way: [z_copy(way, 0, g)])
        start(xs, lambda way: [corner_copy(way, g)])

    def forward_first(g, carry):
        forward(g)
        return carry

    @pl.when(first)
    def _():
        lax.fori_loop(0, GROUPS, forward_first, 0)

    def outer(g, carry):
        @pl.when(jnp.logical_not(first))
        def _():
            forward(g)

        arrived(xs, lambda way: [x_copy(way, g)])
        strips(g)
        outer_rows(0, g, wide0a, left0a)
        put0(left0a, g, 0, 28)
        outer_rows(1, g, wide1a, left1a)
        put1(left1a, g, 0, 12)
        outer_rows(2, g, wide2, left2)
        part2[g] = product(left2[...], 2, g)
        return carry

    lax.fori_loop(0, GROUPS, outer, 0)

    groups = range(GROUPS)
    sent(xs, lambda way: [x_copy(way, g) for g in groups] + [corner_copy(way, g) for g in groups])
    sent(zs, lambda way: [z_copy(way, part, g) for part in range(2) for g in groups])

    first_row = (0, 32, 48)

    def edge_lines(level, g, n):
        block = jnp.concatenate(
            [(z_in if near_z else halo)[g, at:at + 4] for near_z, at in UNITS[level][2 * n:2 * n + 4]], axis=0)
        lines = along_x(block, level, g)
        at = first_row[level] + 8 * n
        twice[at:at + 8, 0:8] = lines
        twice[at:at + 8, 8:16] = lines
        added = line_sum([twice[at:at + 8, j:j + 8] for j in range(1, 8)],
                         [coef[level, g, j - 1] for j in range(1, 8)])
        split_into(left_edge, 8 * at, added)

    def edge(level, g):
        at = 8 * first_row[level]
        return product(left_edge[at:at + 8 * SIZES[level]], level, g)

    low8 = lax.broadcasted_iota(jnp.int32, (8, 8, LANES), 1) < HALF

    def edges(g, carry):
        arrived(zs, lambda way: [z_copy(way, 1, g)])
        edge_lines(0, g, 1)
        edge_lines(0, g, 2)
        derive(g)
        arrived(xs, lambda way: [corner_copy(way, g)])
        edge_lines(2, g, 0)
        total2 = part2[g] + edge(2, g)
        up2[:, pl.ds(0, 8, stride=2)] = total2
        up2[:, pl.ds(1, 8, stride=2)] = total2
        edge_lines(1, g, 0)
        edge_lines(1, g, 1)
        edge1 = edge(1, g)
        for n in range(2):
            mine = edge1[8 * n:8 * n + 8]
            for t in range(2):
                coarse = up2[4 * n:4 * n + 4, 8 * t:8 * t + 8]
                both = jnp.broadcast_to(coarse[:, None], (4, 2, 8, LANES)).reshape(8, 8, LANES)
                side = jnp.where(low8, mine, 0.0) if t == 0 else jnp.where(low8, 0.0, mine)
                total1 = part1[g, 8 * n:8 * n + 8, 8 * t:8 * t + 8] + side + both
                up1[8 * n:8 * n + 8, pl.ds(16 * t, 8, stride=2)] = total1
                up1[8 * n:8 * n + 8, pl.ds(16 * t + 1, 8, stride=2)] = total1
        edge_lines(0, g, 0)
        edge_lines(0, g, 3)
        edge0 = edge(0, g)
        for n in range(4):
            mine = edge0[8 * n:8 * n + 8]
            for t in range(4):
                coarse = up1[4 * n:4 * n + 4, 8 * t:8 * t + 8]
                total = jnp.broadcast_to(coarse[:, None], (4, 2, 8, LANES)).reshape(8, 8, LANES)
                if t == 0:
                    total = total + jnp.where(low8, mine, 0.0)
                if t == 3:
                    total = total + jnp.where(low8, 0.0, mine)
                out[8 * n:8 * n + 8, 8 * t:8 * t + 8, lanes(g)] += total
        return carry

    lax.fori_loop(0, GROUPS, edges, 0)


def solution(mesh):
    nx, ny = mesh.shape["gx"], mesh.shape["gy"]
    hbm = pltpu.MemorySpace.HBM

    def body(field, vertical, horiz_kernel, gen_weight):
        def f32(*shape):
            return pltpu.VMEM(shape, F32)

        def bf16(rows):
            return pltpu.VMEM((rows, 2 * LANES), BF16)

        operands = (field, vertical, jnp.transpose(horiz_kernel, (0, 2, 1, 3)), gen_weight)
        return pl.pallas_call(
            functools.partial(kernel, nx, ny),
            out_shape=jax.ShapeDtypeStruct(field.shape, F32),
            in_specs=[pl.BlockSpec(memory_space=hbm)] * 4,
            out_specs=pl.BlockSpec(memory_space=pltpu.MemorySpace.VMEM),
            scratch_shapes=[
                f32(GROUPS, 32, 32, LANES), f32(GROUPS, 16, 16, LANES), f32(GROUPS, 8, 8, LANES),
                f32(2, GROUPS, STRIP[3], 8, LANES), f32(2, GROUPS, STRIP[3], 8, LANES),
                f32(GROUPS, 52, 8, LANES), f32(GROUPS, 52, 8, LANES), f32(GROUPS, ROWS, 8, LANES),
                f32(8, 48, LANES), f32(8, 48, LANES), f32(8, 48, LANES),
                f32(8, 32, LANES), f32(8, 24, LANES), f32(2, 4, 16, LANES), f32(2, 4, 8, LANES),
                f32(*vertical.shape), f32(GENS, VARS, 2, TAPS), f32(*gen_weight.shape),
                f32(GENS, GROUPS * LANES),
                f32(GENS, 2, GROUPS, TAPS, 8, LANES), f32(GENS, GROUPS, 7, 8, LANES),
                f32(LANES, LANES), pltpu.VMEM((GENS, GROUPS, 2 * LANES, 2 * LANES), BF16),
                f32(16, 32, LANES), f32(2, 32, LANES),
                bf16(256), bf16(256), bf16(256), bf16(128), bf16(64), f32(56, 16, LANES), bf16(448),
                f32(GROUPS, 16, 16, LANES), f32(GROUPS, 8, 8, LANES), f32(16, 32, LANES), f32(8, 16, LANES),
                pltpu.SemaphoreType.DMA((GROUPS + 3,)),
                pltpu.SemaphoreType.DMA((24,)),
                pltpu.SemaphoreType.DMA((24,)),
                pltpu.SemaphoreType.REGULAR,
            ],
            compiler_params=pltpu.CompilerParams(
                collective_id=0, has_side_effects=True, vmem_limit_bytes=40 * 2 ** 20),
        )(*[pltpu.with_memory_space_constraint(operand, hbm) for operand in operands])

    return jax.shard_map(
        body, mesh=mesh, in_specs=(P("gx", "gy", None), P(), P(), P()),
        out_specs=P("gx", "gy", None), check_vma=False)
```

```python
import functools

import jax
import jax.numpy as jnp
from jax import lax
from jax.experimental import pallas as pl
from jax.experimental.pallas import tpu as pltpu
from jax.sharding import PartitionSpec as P

GENS = 3
HALF = 4
TAPS = 9
VARS = 6
LEVELS = 64
LANES = 128
GROUPS = 3
SIZES = (32, 16, 8)
MESH = pl.DeviceIdType.MESH
F32 = jnp.float32
BF16 = jnp.bfloat16

STRIP = (0, 16, 20, 22)
FIRST, SECOND = (0, 24), (24, 28)
RING = 48
BELOW, ABOVE, MIDDLE, ROWS = 0, 12, 24, 32
UNITS = (
    ((0, 0), (1, 0), (1, 24), (1, 28), (1, 32), (1, 36), (1, 40), (1, 44), (1, 12), (0, 12)),
    ((0, 4), (1, 4), (0, 24), (0, 28), (1, 16), (0, 16)),
    ((0, 8), (1, 8), (1, 20), (0, 20)),
)


def line_sum(pieces, taps):
    total = taps[0] * pieces[0]
    for piece, tap in zip(pieces[1:], taps[1:]):
        total = total + tap * piece
    return total


def split_into(ref, at, values):
    rows = values.shape[0] * values.shape[1]
    flat = values.reshape(rows, LANES)
    head = flat.astype(BF16)
    ref[at:at + rows, 0:LANES] = head
    ref[at:at + rows, LANES:] = (flat - head.astype(F32)).astype(BF16)


def kernel(nx, ny, field, vertical, horiz, weight, out,
           grid0, grid1, grid2, x_out, x_in, z_out, z_in, halo,
           wide0a, wide0b, wide0c, wide1a, wide2, strip1, strip2,
           vert, hk, gw, scale, taps, coef, wfull, mats, pair, quad,
           left0a, left0b, left0c, left1a, left2, twice, left_edge, part1, part2, up1, up2,
           load_sem, send_sem, recv_sem, corner_ready):
    gx, gy = lax.axis_index("gx"), lax.axis_index("gy")
    grids = (grid0, grid1, grid2)

    has = {"xl": gx > 0, "xr": gx < nx - 1, "zl": gy > 0, "zr": gy < ny - 1}
    ids = {"xl": {"gx": gx - 1}, "xr": {"gx": gx + 1}, "zl": {"gy": gy - 1}, "zr": {"gy": gy + 1}}
    back = {"xl": "xr", "xr": "xl", "zl": "zr", "zr": "zl"}
    xs, zs = ("xl", "xr"), ("zl", "zr")

    first = (gx == 0) & (gy == 0)
    near = {"xl": (gx == 1) & (gy == 0), "zl": (gx == 0) & (gy == 1)}
    now = {way: has[way] & jnp.logical_not(near[way]) if way in near else has[way] for way in has}

    barrier = pltpu.get_barrier_semaphore()
    for way in has:
        @pl.when(has[way] & jnp.logical_not(first))
        def _(way=way):
            pl.semaphore_signal(barrier, inc=1, device_id=ids[way], device_id_type=MESH)

    @pl.when(first)
    def _():
        pl.semaphore_wait(barrier, 2)
        for way in ("xr", "zr"):
            pl.semaphore_signal(corner_ready, inc=1, device_id=ids[way], device_id_type=MESH)

    small = [
        pltpu.make_async_copy(src, dst, load_sem.at[GROUPS + n])
        for n, (src, dst) in enumerate(((horiz, hk), (weight, gw), (vertical, vert)))
    ]
    loads = [
        pltpu.make_async_copy(field.at[:, :, pl.ds(g * LANES, LANES)], grid0.at[g], load_sem.at[g])
        for g in range(GROUPS)
    ]
    for load in small[:2] + loads + small[2:]:
        load.start()

    for way in has:
        @pl.when(jnp.logical_not(has[way]))
        def _(way=way):
            if way in xs:
                x_in[xs.index(way)] = jnp.zeros((GROUPS, STRIP[3], 8, LANES), F32)
                at = BELOW if way == "xl" else ABOVE
                halo[:, at:at + 12] = jnp.zeros((GROUPS, 12, 8, LANES), F32)
            else:
                at = HALF if way == "zl" else 0
                z_in[:, :, at:at + HALF] = jnp.zeros((GROUPS, 52, HALF, LANES), F32)
    for wide, size in ((wide0a, 32), (wide0b, 32), (wide0c, 32), (wide1a, 16), (wide2, 8)):
        wide[:, 0:8] = jnp.zeros((8, 8, LANES), F32)
        wide[:, size + 8:] = jnp.zeros((8, 8, LANES), F32)

    def remote(way, src, dst, slot):
        return pltpu.make_async_remote_copy(
            src_ref=src, dst_ref=dst, send_sem=send_sem.at[slot], recv_sem=recv_sem.at[slot],
            device_id=ids[way], device_id_type=MESH)

    def x_copy(way, g):
        n = xs.index(way)
        return remote(way, x_out.at[n, g], x_in.at[1 - n, g], n * 3 + g)

    def z_copy(way, part, g):
        start, rows = (FIRST, SECOND)[part]
        cols = pl.ds(zs.index(way) * HALF, HALF)
        return remote(way, z_out.at[g, pl.ds(start, rows), cols], z_in.at[g, pl.ds(start, rows), cols],
                      6 + part * 6 + zs.index(way) * 3 + g)

    def corner_copy(way, g):
        here, there = (0, ABOVE) if way == "xl" else (12, BELOW)
        return remote(way, z_in.at[g, pl.ds(here, 12)], halo.at[g, pl.ds(there, 12)],
                      18 + xs.index(way) * 3 + g)

    def start(ways, make, gate=has):
        for way in ways:
            @pl.when(gate[way])
            def _(way=way):
                for copy in make(way):
                    copy.start()

    def arrived(ways, make):
        for way in ways:
            @pl.when(has[back[way]])
            def _(way=way):
                for copy in make(way):
                    copy.wait_recv()

    def sent(ways, make):
        for way in ways:
            @pl.when(has[way])
            def _(way=way):
                for copy in make(way):
                    copy.wait_send()

    lower = lax.broadcasted_iota(jnp.int32, (4, 8, LANES), 1) < HALF

    def prepare(g, carry):
        for fine, coarse, size in ((grid0, grid1, 16), (grid1, grid2, 8)):
            for r in range(size):
                pair[r, 0:2 * size] = fine[g, 2 * r] + fine[g, 2 * r + 1]
                coarse[g, r] = 0.25 * (
                    pair[r, pl.ds(0, size, stride=2)] + pair[r, pl.ds(1, size, stride=2)])
        for level, size in enumerate(SIZES):
            rows = ((0, 4), (size - 4, size)) if level == 0 else ((2, 4), (size - 4, size - 2))
            for n, (low, high) in enumerate(rows):
                x_out[n, g, STRIP[level]:STRIP[level + 1]] = grids[level][g, low:high].reshape(-1, 8, LANES)
        for level, here, there in (
                (0, 0, 0), (1, 0, 4), (2, 0, 8), (0, 28, 12), (1, 12, 16), (2, 4, 20),
                (0, 4, 24), (0, 8, 28), (0, 12, 32), (0, 16, 36), (0, 20, 40), (0, 24, 44)):
            size, rows = SIZES[level], pl.ds(here, 4)
            head, tail = grids[level][g, rows, 0:8], grids[level][g, rows, size - 8:size]
            z_out[g, there:there + 4] = jnp.where(lower, head, tail)
        for k in range(4):
            for odd in range(2):
                z_out[g, RING + k, 2 * odd:2 * odd + 2] = grid1[g, 4 + 2 * k + odd, 2:4]
                z_out[g, RING + k, 4 + 2 * odd:6 + 2 * odd] = grid1[g, 4 + 2 * k + odd, 12:14]
        return carry

    small[0].wait()
    small[1].wait()
    lane = lax.broadcasted_iota(jnp.int32, (VARS, GROUPS * LANES), 1)
    row = lax.broadcasted_iota(jnp.int32, (VARS, GROUPS * LANES), 0)
    pick = jnp.where((lane >= row * LEVELS) & (lane < (row + 1) * LEVELS), 1.0, 0.0).astype(F32)
    col = lax.broadcasted_iota(jnp.int32, (8, LANES), 0)
    for level in range(GENS):
        for axis in range(2):
            raw = hk[level, :, axis]
            norm = raw / jnp.sum(raw, axis=-1, keepdims=True)
            spread = lax.dot_general(norm, pick, (((0,), (0,)), ((), ())),
                                     precision=lax.Precision.HIGHEST, preferred_element_type=F32)
            for g in range(GROUPS):
                for step in range(TAPS):
                    taps[level, axis, g, step] = jnp.broadcast_to(
                        spread[step:step + 1, g * LANES:(g + 1) * LANES], (8, LANES))
        for g in range(GROUPS):
            for j in range(1, 8):
                right = taps[level, 1, g, HALF + j] if j <= HALF else 0.0
                left = taps[level, 1, g, j - HALF] if j >= HALF else 0.0
                coef[level, g, j - 1] = jnp.where(col >= 8 - j, right, left)
    scale[...] = jnp.dot(gw[...], pick, precision=lax.Precision.HIGHEST, preferred_element_type=F32)

    def matrices():
        small[2].wait()
        wfull[...] = jnp.zeros_like(wfull)
        for level in range(GENS):
            for g in range(GROUPS):
                wfull[0:LEVELS, 0:LEVELS] = vert[level, 2 * g]
                wfull[LEVELS:LANES, LEVELS:LANES] = vert[level, 2 * g + 1]
                whole = wfull[...] * scale[level:level + 1, g * LANES:(g + 1) * LANES]
                head = whole.astype(BF16)
                tail = (whole - head.astype(F32)).astype(BF16)
                for at in (0, LANES):
                    mats[level, g, at:at + LANES, 0:LANES] = head
                    mats[level, g, at:at + LANES, LANES:] = tail

    for g in range(GROUPS):
        loads[g].wait()
    lax.fori_loop(0, GROUPS, prepare, 0)

    @pl.when(jnp.logical_not(first))
    def _():
        pl.semaphore_wait(barrier, sum(flag.astype(jnp.int32) for flag in now.values()))

    start(zs, lambda way: [z_copy(way, 0, g) for g in range(GROUPS)], now)
    start(xs, lambda way: [x_copy(way, g) for g in range(GROUPS)], now)
    start(zs, lambda way: [z_copy(way, 1, g) for g in range(GROUPS)], now)
    matrices()

    def along_x(block, level, g):
        ktaps = [taps[level, 0, g, step] for step in range(TAPS)]
        count = block.shape[0] - 2 * HALF
        return line_sum([block[step:step + count] for step in range(TAPS)], ktaps)

    def along_y(level, g, wide, left):
        ktaps = [taps[level, 1, g, step] for step in range(TAPS)]
        for t in range(SIZES[level] // 8):
            at = 8 * t + HALF
            split_into(left, 64 * t, line_sum([wide[:, at + s:at + s + 8] for s in range(TAPS)], ktaps))

    def strips(g):
        for side in range(2):
            for level, fine, size in ((1, x_in, 16), (2, strip1, 8)):
                strip, tiles = (strip1, strip2)[level - 1], size // 8
                for r in range(2):
                    own, ring = (2 + r, r) if side == 0 else (r, 2 + r)
                    for t in range(2 * tiles):
                        if level == 1:
                            both = x_in[side, g, 8 * r + t] + x_in[side, g, 8 * r + 4 + t]
                        else:
                            both = strip1[side, 2 * r, 8 * t:8 * t + 8] + strip1[side, 2 * r + 1, 8 * t:8 * t + 8]
                        pair[2 * side + r, 8 * t:8 * t + 8] = both
                    strip[side, own] = 0.25 * (
                        pair[2 * side + r, pl.ds(0, size, stride=2)] + pair[2 * side + r, pl.ds(1, size, stride=2)])
                    for t in range(tiles):
                        strip[side, ring, 8 * t:8 * t + 8] = x_in[side, g, STRIP[level] + r * tiles + t]

    def strip(side, level, g, t):
        if level == 0:
            return jnp.concatenate([x_in[side, g, pl.ds(4 * r + t, 1)] for r in range(HALF)], axis=0)
        return (strip1, strip2)[level - 1][side, :, 8 * t:8 * t + 8]

    def inner_rows(level, g, row, wide, left):
        for t in range(SIZES[level] // 8):
            wide[:, 8 + 8 * t:16 + 8 * t] = along_x(
                grids[level][g, row - HALF:row + 12, 8 * t:8 * t + 8], level, g)
        along_y(level, g, wide, left)

    def outer_rows(level, g, wide, left):
        size = SIZES[level]
        for t in range(size // 8):
            cols, to = slice(8 * t, 8 * t + 8), slice(8 + 8 * t, 16 + 8 * t)
            low, high = strip(0, level, g, t), strip(1, level, g, t)
            if level == 2:
                wide[:, to] = along_x(jnp.concatenate([low, grid2[g], high], axis=0), level, g)
            else:
                wide[0:4, to] = along_x(jnp.concatenate([low, grids[level][g, 0:8, cols]], axis=0), level, g)
                wide[4:8, to] = along_x(
                    jnp.concatenate([grids[level][g, size - 8:size, cols], high], axis=0), level, g)
        along_y(level, g, wide, left)

    def product(left, level, g):
        both = jnp.dot(left, mats[level, g], preferred_element_type=F32)
        total = both[:, 0:LANES] + both[:, LANES:]
        return total.reshape(total.shape[0] // 8, 8, LANES)

    def lanes(g):
        return pl.ds(pl.multiple_of(g * LANES, LANES), LANES)

    def put0(left, g, low, high):
        total = product(left[...], 0, g)
        for t in range(4):
            out[low:low + 4, 8 * t:8 * t + 8, lanes(g)] = total[8 * t:8 * t + 4]
            out[high:high + 4, 8 * t:8 * t + 8, lanes(g)] = total[8 * t + 4:8 * t + 8]

    def put1(left, g, low, high):
        total = product(left[...], 1, g)
        for t in range(2):
            part1[g, low:low + 4, 8 * t:8 * t + 8] = total[8 * t:8 * t + 4]
            part1[g, high:high + 4, 8 * t:8 * t + 8] = total[8 * t + 4:8 * t + 8]

    def inner_four(g):
        inner_rows(0, g, 4, wide0a, left0a)
        put0(left0a, g, 4, 8)
        inner_rows(0, g, 12, wide0b, left0b)
        put0(left0b, g, 12, 16)
        inner_rows(1, g, 4, wide1a, left1a)
        put1(left1a, g, 4, 8)
        inner_rows(0, g, 20, wide0c, left0c)

    def inner(g, carry):
        put0(left0c, g - 1, 20, 24)
        inner_four(g)
        return carry

    inner_four(0)
    lax.fori_loop(1, GROUPS, inner, 0)
    put0(left0c, GROUPS - 1, 20, 24)

    for way in near:
        @pl.when(near[way])
        def _(way=way):
            pl.semaphore_wait(corner_ready, 1)
            if way == "xl":
                copies = [x_copy(way, g) for g in range(GROUPS)]
            else:
                copies = [z_copy(way, part, g) for part in range(2) for g in range(GROUPS)]
            for copy in copies:
                copy.start()

    def derive(g):
        for k in range(2):
            rows = z_in[g, 28 + 8 * k:36 + 8 * k].reshape(4, 2, 8, LANES)
            quad[k] = (rows[:, 0] + rows[:, 1]).reshape(32, LANES)
            means = 0.25 * (quad[k, pl.ds(0, 16, stride=2)] + quad[k, pl.ds(1, 16, stride=2)])
            for r in range(4):
                at, ring, odd = MIDDLE + 4 * k + r, RING + 2 * k + r // 2, r % 2
                halo[g, at, 0:2] = means[4 * r:4 * r + 2]
                halo[g, at, 6:8] = means[4 * r + 2:4 * r + 4]
                halo[g, at, 2:4] = z_in[g, ring, 2 * odd:2 * odd + 2]
                halo[g, at, 4:6] = z_in[g, ring, 4 + 2 * odd:6 + 2 * odd]

    def forward(g):
        arrived(zs, lambda way: [z_copy(way, 0, g)])
        start(xs, lambda way: [corner_copy(way, g)])

    def forward_first(g, carry):
        forward(g)
        return carry

    @pl.when(first)
    def _():
        lax.fori_loop(0, GROUPS, forward_first, 0)

    def outer(g, carry):
        arrived(xs, lambda way: [x_copy(way, g)])
        strips(g)
        outer_rows(0, g, wide0a, left0a)
        put0(left0a, g, 0, 28)
        outer_rows(1, g, wide1a, left1a)
        put1(left1a, g, 0, 12)
        outer_rows(2, g, wide2, left2)
        part2[g] = product(left2[...], 2, g)
        return carry

    def forward_then_outer(g, carry):
        @pl.when(jnp.logical_not(first) & (g < GROUPS))
        def _():
            forward(jnp.minimum(g, GROUPS - 1))

        return outer(g - 1, carry)

    @pl.when(jnp.logical_not(first))
    def _():
        forward(0)

    lax.fori_loop(1, GROUPS + 1, forward_then_outer, 0)

    groups = range(GROUPS)
    sent(xs, lambda way: [x_copy(way, g) for g in groups] + [corner_copy(way, g) for g in groups])
    sent(zs, lambda way: [z_copy(way, part, g) for part in range(2) for g in groups])

    first_row = (0, 32, 48)

    def edge_lines(level, g, unit):
        block = jnp.concatenate(
            [(z_in if near_z else halo)[g, at:at + 4] for near_z, at in UNITS[level][unit:unit + 3]], axis=0)
        lines = along_x(block, level, g)
        at = first_row[level] + 4 * unit
        twice[at:at + 4, 0:8] = lines
        twice[at:at + 4, 8:16] = lines
        added = line_sum([twice[at:at + 4, j:j + 8] for j in range(1, 8)],
                         [coef[level, g, j - 1] for j in range(1, 8)])
        split_into(left_edge, 8 * at, added)

    def edge(level, g):
        at = 8 * first_row[level]
        return product(left_edge[at:at + 8 * SIZES[level]], level, g)

    low8 = lax.broadcasted_iota(jnp.int32, (8, 8, LANES), 1) < HALF

    def edges(g, carry):
        arrived(zs, lambda way: [z_copy(way, 1, g)])
        for unit in range(1, 7):
            edge_lines(0, g, unit)
        derive(g)
        edge_lines(1, g, 1)
        edge_lines(1, g, 2)
        arrived(xs, lambda way: [corner_copy(way, g)])
        edge_lines(2, g, 0)
        edge_lines(2, g, 1)
        total2 = part2[g] + edge(2, g)
        up2[:, pl.ds(0, 8, stride=2)] = total2
        up2[:, pl.ds(1, 8, stride=2)] = total2
        edge_lines(1, g, 0)
        edge_lines(1, g, 3)
        edge1 = edge(1, g)
        for n in range(2):
            mine = edge1[8 * n:8 * n + 8]
            for t in range(2):
                coarse = up2[4 * n:4 * n + 4, 8 * t:8 * t + 8]
                both = jnp.broadcast_to(coarse[:, None], (4, 2, 8, LANES)).reshape(8, 8, LANES)
                side = jnp.where(low8, mine, 0.0) if t == 0 else jnp.where(low8, 0.0, mine)
                total1 = part1[g, 8 * n:8 * n + 8, 8 * t:8 * t + 8] + side + both
                up1[8 * n:8 * n + 8, pl.ds(16 * t, 8, stride=2)] = total1
                up1[8 * n:8 * n + 8, pl.ds(16 * t + 1, 8, stride=2)] = total1
        edge_lines(0, g, 0)
        edge_lines(0, g, 7)
        edge0 = edge(0, g)
        for n in range(4):
            mine = edge0[8 * n:8 * n + 8]
            for t in range(4):
                coarse = up1[4 * n:4 * n + 4, 8 * t:8 * t + 8]
                total = jnp.broadcast_to(coarse[:, None], (4, 2, 8, LANES)).reshape(8, 8, LANES)
                if t == 0:
                    total = total + jnp.where(low8, mine, 0.0)
                if t == 3:
                    total = total + jnp.where(low8, 0.0, mine)
                out[8 * n:8 * n + 8, 8 * t:8 * t + 8, lanes(g)] += total
        return carry

    lax.fori_loop(0, GROUPS, edges, 0)


def solution(mesh):
    nx, ny = mesh.shape["gx"], mesh.shape["gy"]
    hbm = pltpu.MemorySpace.HBM

    def body(field, vertical, horiz_kernel, gen_weight):
        def f32(*shape):
            return pltpu.VMEM(shape, F32)

        def bf16(rows):
            return pltpu.VMEM((rows, 2 * LANES), BF16)

        operands = (field, vertical, jnp.transpose(horiz_kernel, (0, 2, 1, 3)), gen_weight)
        return pl.pallas_call(
            functools.partial(kernel, nx, ny),
            out_shape=jax.ShapeDtypeStruct(field.shape, F32),
            in_specs=[pl.BlockSpec(memory_space=hbm)] * 4,
            out_specs=pl.BlockSpec(memory_space=pltpu.MemorySpace.VMEM),
            scratch_shapes=[
                f32(GROUPS, 32, 32, LANES), f32(GROUPS, 16, 16, LANES), f32(GROUPS, 8, 8, LANES),
                f32(2, GROUPS, STRIP[3], 8, LANES), f32(2, GROUPS, STRIP[3], 8, LANES),
                f32(GROUPS, 52, 8, LANES), f32(GROUPS, 52, 8, LANES), f32(GROUPS, ROWS, 8, LANES),
                f32(8, 48, LANES), f32(8, 48, LANES), f32(8, 48, LANES),
                f32(8, 32, LANES), f32(8, 24, LANES), f32(2, 4, 16, LANES), f32(2, 4, 8, LANES),
                f32(*vertical.shape), f32(GENS, VARS, 2, TAPS), f32(*gen_weight.shape),
                f32(GENS, GROUPS * LANES),
                f32(GENS, 2, GROUPS, TAPS, 8, LANES), f32(GENS, GROUPS, 7, 8, LANES),
                f32(LANES, LANES), pltpu.VMEM((GENS, GROUPS, 2 * LANES, 2 * LANES), BF16),
                f32(16, 32, LANES), f32(2, 32, LANES),
                bf16(256), bf16(256), bf16(256), bf16(128), bf16(64), f32(56, 16, LANES), bf16(448),
                f32(GROUPS, 16, 16, LANES), f32(GROUPS, 8, 8, LANES), f32(16, 32, LANES), f32(8, 16, LANES),
                pltpu.SemaphoreType.DMA((GROUPS + 3,)),
                pltpu.SemaphoreType.DMA((24,)),
                pltpu.SemaphoreType.DMA((24,)),
                pltpu.SemaphoreType.REGULAR,
            ],
            compiler_params=pltpu.CompilerParams(
                collective_id=0, has_side_effects=True, vmem_limit_bytes=40 * 2 ** 20),
        )(*[pltpu.with_memory_space_constraint(operand, hbm) for operand in operands])

    return jax.shard_map(
        body, mesh=mesh, in_specs=(P("gx", "gy", None), P(), P(), P()),
        out_specs=P("gx", "gy", None), check_vma=False)
```

```python
import functools

import jax
import jax.numpy as jnp
from jax import lax
from jax.experimental import pallas as pl
from jax.experimental.pallas import tpu as pltpu
from jax.sharding import PartitionSpec as P

GENS = 3
HALF = 4
TAPS = 9
VARS = 6
LEVELS = 64
LANES = 128
GROUPS = 3
SIZES = (32, 16, 8)
MESH = pl.DeviceIdType.MESH
F32 = jnp.float32
BF16 = jnp.bfloat16

STRIP = (0, 16, 20, 22)
FIRST, SECOND = (0, 24), (24, 28)
RING = 48
BELOW, ABOVE, MIDDLE, ROWS = 0, 12, 24, 32
UNITS = (
    ((0, 0), (1, 0), (1, 24), (1, 28), (1, 32), (1, 36), (1, 40), (1, 44), (1, 12), (0, 12)),
    ((0, 4), (1, 4), (0, 24), (0, 28), (1, 16), (0, 16)),
    ((0, 8), (1, 8), (1, 20), (0, 20)),
)


def line_sum(pieces, taps):
    total = taps[0] * pieces[0]
    for piece, tap in zip(pieces[1:], taps[1:]):
        total = total + tap * piece
    return total


def split_into(ref, at, values):
    rows = values.shape[0] * values.shape[1]
    flat = values.reshape(rows, LANES)
    head = flat.astype(BF16)
    ref[at:at + rows, 0:LANES] = head
    ref[at:at + rows, LANES:] = (flat - head.astype(F32)).astype(BF16)


def kernel(nx, ny, field, vertical, horiz, weight, out,
           grid0, grid1, grid2, x_out, x_in, z_out, z_in, halo,
           wide0a, wide0b, wide0c, wide1a, wide2, strip1, strip2,
           vert, hk, gw, scale, taps, coef, wfull, mats, pair, quad,
           left0a, left0b, left0c, left1a, left2, twice, left_edge, part1, part2, up1, up2,
           load_sem, send_sem, recv_sem, corner_ready):
    gx, gy = lax.axis_index("gx"), lax.axis_index("gy")
    grids = (grid0, grid1, grid2)

    has = {"xl": gx > 0, "xr": gx < nx - 1, "zl": gy > 0, "zr": gy < ny - 1}
    ids = {"xl": {"gx": gx - 1}, "xr": {"gx": gx + 1}, "zl": {"gy": gy - 1}, "zr": {"gy": gy + 1}}
    back = {"xl": "xr", "xr": "xl", "zl": "zr", "zr": "zl"}
    xs, zs = ("xl", "xr"), ("zl", "zr")

    first = (gx == 0) & (gy == 0)
    near = {"xl": (gx == 1) & (gy == 0), "zl": (gx == 0) & (gy == 1)}
    now = {way: has[way] & jnp.logical_not(near[way]) if way in near else has[way] for way in has}

    barrier = pltpu.get_barrier_semaphore()
    for way in has:
        @pl.when(has[way] & jnp.logical_not(first))
        def _(way=way):
            pl.semaphore_signal(barrier, inc=1, device_id=ids[way], device_id_type=MESH)

    @pl.when(first)
    def _():
        pl.semaphore_wait(barrier, 2)
        for way in ("xr", "zr"):
            pl.semaphore_signal(corner_ready, inc=1, device_id=ids[way], device_id_type=MESH)

    small = [
        pltpu.make_async_copy(src, dst, load_sem.at[GROUPS + n])
        for n, (src, dst) in enumerate(((horiz, hk), (weight, gw), (vertical, vert)))
    ]
    loads = [
        pltpu.make_async_copy(field.at[:, :, pl.ds(g * LANES, LANES)], grid0.at[g], load_sem.at[g])
        for g in range(GROUPS)
    ]
    for load in small[:2] + loads + small[2:]:
        load.start()

    for way in has:
        @pl.when(jnp.logical_not(has[way]))
        def _(way=way):
            if way in xs:
                x_in[xs.index(way)] = jnp.zeros((GROUPS, STRIP[3], 8, LANES), F32)
                at = BELOW if way == "xl" else ABOVE
                halo[:, at:at + 12] = jnp.zeros((GROUPS, 12, 8, LANES), F32)
            else:
                at = HALF if way == "zl" else 0
                z_in[:, :, at:at + HALF] = jnp.zeros((GROUPS, 52, HALF, LANES), F32)
    for wide, size in ((wide0a, 32), (wide0b, 32), (wide0c, 32), (wide1a, 16), (wide2, 8)):
        wide[:, 0:8] = jnp.zeros((8, 8, LANES), F32)
        wide[:, size + 8:] = jnp.zeros((8, 8, LANES), F32)

    def remote(way, src, dst, slot):
        return pltpu.make_async_remote_copy(
            src_ref=src, dst_ref=dst, send_sem=send_sem.at[slot], recv_sem=recv_sem.at[slot],
            device_id=ids[way], device_id_type=MESH)

    def x_copy(way, g):
        n = xs.index(way)
        return remote(way, x_out.at[n, g], x_in.at[1 - n, g], n * 3 + g)

    def z_copy(way, part, g):
        start, rows = (FIRST, SECOND)[part]
        cols = pl.ds(zs.index(way) * HALF, HALF)
        return remote(way, z_out.at[g, pl.ds(start, rows), cols], z_in.at[g, pl.ds(start, rows), cols],
                      6 + part * 6 + zs.index(way) * 3 + g)

    def corner_copy(way, g):
        here, there = (0, ABOVE) if way == "xl" else (12, BELOW)
        return remote(way, z_in.at[g, pl.ds(here, 12)], halo.at[g, pl.ds(there, 12)],
                      18 + xs.index(way) * 3 + g)

    def start(ways, make, gate=has):
        for way in ways:
            @pl.when(gate[way])
            def _(way=way):
                for copy in make(way):
                    copy.start()

    def arrived(ways, make):
        for way in ways:
            @pl.when(has[back[way]])
            def _(way=way):
                for copy in make(way):
                    copy.wait_recv()

    def sent(ways, make):
        for way in ways:
            @pl.when(has[way])
            def _(way=way):
                for copy in make(way):
                    copy.wait_send()

    lower = lax.broadcasted_iota(jnp.int32, (4, 8, LANES), 1) < HALF

    def prepare(g, carry):
        for fine, coarse, size in ((grid0, grid1, 16), (grid1, grid2, 8)):
            for r in range(size):
                pair[r, 0:2 * size] = fine[g, 2 * r] + fine[g, 2 * r + 1]
                coarse[g, r] = 0.25 * (
                    pair[r, pl.ds(0, size, stride=2)] + pair[r, pl.ds(1, size, stride=2)])
        for level, size in enumerate(SIZES):
            rows = ((0, 4), (size - 4, size)) if level == 0 else ((2, 4), (size - 4, size - 2))
            for n, (low, high) in enumerate(rows):
                x_out[n, g, STRIP[level]:STRIP[level + 1]] = grids[level][g, low:high].reshape(-1, 8, LANES)
        for level, here, there in (
                (0, 0, 0), (1, 0, 4), (2, 0, 8), (0, 28, 12), (1, 12, 16), (2, 4, 20),
                (0, 4, 24), (0, 8, 28), (0, 12, 32), (0, 16, 36), (0, 20, 40), (0, 24, 44)):
            size, rows = SIZES[level], pl.ds(here, 4)
            head, tail = grids[level][g, rows, 0:8], grids[level][g, rows, size - 8:size]
            z_out[g, there:there + 4] = jnp.where(lower, head, tail)
        for k in range(4):
            for odd in range(2):
                z_out[g, RING + k, 2 * odd:2 * odd + 2] = grid1[g, 4 + 2 * k + odd, 2:4]
                z_out[g, RING + k, 4 + 2 * odd:6 + 2 * odd] = grid1[g, 4 + 2 * k + odd, 12:14]
        return carry

    small[0].wait()
    small[1].wait()
    lane = lax.broadcasted_iota(jnp.int32, (VARS, GROUPS * LANES), 1)
    row = lax.broadcasted_iota(jnp.int32, (VARS, GROUPS * LANES), 0)
    pick = jnp.where((lane >= row * LEVELS) & (lane < (row + 1) * LEVELS), 1.0, 0.0).astype(F32)
    col = lax.broadcasted_iota(jnp.int32, (8, LANES), 0)
    for level in range(GENS):
        for axis in range(2):
            raw = hk[level, :, axis]
            norm = raw / jnp.sum(raw, axis=-1, keepdims=True)
            spread = lax.dot_general(norm, pick, (((0,), (0,)), ((), ())),
                                     precision=lax.Precision.HIGHEST, preferred_element_type=F32)
            for g in range(GROUPS):
                for step in range(TAPS):
                    taps[level, axis, g, step] = jnp.broadcast_to(
                        spread[step:step + 1, g * LANES:(g + 1) * LANES], (8, LANES))
        for g in range(GROUPS):
            for j in range(1, 8):
                right = taps[level, 1, g, HALF + j] if j <= HALF else 0.0
                left = taps[level, 1, g, j - HALF] if j >= HALF else 0.0
                coef[level, g, j - 1] = jnp.where(col >= 8 - j, right, left)
    scale[...] = jnp.dot(gw[...], pick, precision=lax.Precision.HIGHEST, preferred_element_type=F32)

    def matrices():
        small[2].wait()
        wfull[...] = jnp.zeros_like(wfull)
        for level in range(GENS):
            for g in range(GROUPS):
                wfull[0:LEVELS, 0:LEVELS] = vert[level, 2 * g]
                wfull[LEVELS:LANES, LEVELS:LANES] = vert[level, 2 * g + 1]
                whole = wfull[...] * scale[level:level + 1, g * LANES:(g + 1) * LANES]
                head = whole.astype(BF16)
                tail = (whole - head.astype(F32)).astype(BF16)
                for at in (0, LANES):
                    mats[level, g, at:at + LANES, 0:LANES] = head
                    mats[level, g, at:at + LANES, LANES:] = tail

    for g in range(GROUPS):
        loads[g].wait()
    lax.fori_loop(0, GROUPS, prepare, 0)

    @pl.when(jnp.logical_not(first))
    def _():
        pl.semaphore_wait(barrier, sum(flag.astype(jnp.int32) for flag in now.values()))

    start(zs, lambda way: [z_copy(way, 0, g) for g in range(GROUPS)], now)
    start(xs, lambda way: [x_copy(way, g) for g in range(GROUPS)], now)
    matrices()

    def along_x(block, level, g):
        ktaps = [taps[level, 0, g, step] for step in range(TAPS)]
        count = block.shape[0] - 2 * HALF
        return line_sum([block[step:step + count] for step in range(TAPS)], ktaps)

    def along_y(level, g, wide, left):
        ktaps = [taps[level, 1, g, step] for step in range(TAPS)]
        for t in range(SIZES[level] // 8):
            at = 8 * t + HALF
            split_into(left, 64 * t, line_sum([wide[:, at + s:at + s + 8] for s in range(TAPS)], ktaps))

    def strips(g):
        for side in range(2):
            for level, fine, size in ((1, x_in, 16), (2, strip1, 8)):
                strip, tiles = (strip1, strip2)[level - 1], size // 8
                for r in range(2):
                    own, ring = (2 + r, r) if side == 0 else (r, 2 + r)
                    for t in range(2 * tiles):
                        if level == 1:
                            both = x_in[side, g, 8 * r + t] + x_in[side, g, 8 * r + 4 + t]
                        else:
                            both = strip1[side, 2 * r, 8 * t:8 * t + 8] + strip1[side, 2 * r + 1, 8 * t:8 * t + 8]
                        pair[2 * side + r, 8 * t:8 * t + 8] = both
                    strip[side, own] = 0.25 * (
                        pair[2 * side + r, pl.ds(0, size, stride=2)] + pair[2 * side + r, pl.ds(1, size, stride=2)])
                    for t in range(tiles):
                        strip[side, ring, 8 * t:8 * t + 8] = x_in[side, g, STRIP[level] + r * tiles + t]

    def strip(side, level, g, t):
        if level == 0:
            return jnp.concatenate([x_in[side, g, pl.ds(4 * r + t, 1)] for r in range(HALF)], axis=0)
        return (strip1, strip2)[level - 1][side, :, 8 * t:8 * t + 8]

    def inner_rows(level, g, row, wide, left):
        for t in range(SIZES[level] // 8):
            wide[:, 8 + 8 * t:16 + 8 * t] = along_x(
                grids[level][g, row - HALF:row + 12, 8 * t:8 * t + 8], level, g)
        along_y(level, g, wide, left)

    def outer_rows(level, g, wide, left):
        size = SIZES[level]
        for t in range(size // 8):
            cols, to = slice(8 * t, 8 * t + 8), slice(8 + 8 * t, 16 + 8 * t)
            low, high = strip(0, level, g, t), strip(1, level, g, t)
            if level == 2:
                wide[:, to] = along_x(jnp.concatenate([low, grid2[g], high], axis=0), level, g)
            else:
                wide[0:4, to] = along_x(jnp.concatenate([low, grids[level][g, 0:8, cols]], axis=0), level, g)
                wide[4:8, to] = along_x(
                    jnp.concatenate([grids[level][g, size - 8:size, cols], high], axis=0), level, g)
        along_y(level, g, wide, left)

    def product(left, level, g):
        both = jnp.dot(left, mats[level, g], preferred_element_type=F32)
        total = both[:, 0:LANES] + both[:, LANES:]
        return total.reshape(total.shape[0] // 8, 8, LANES)

    def lanes(g):
        return pl.ds(pl.multiple_of(g * LANES, LANES), LANES)

    def put0(left, g, low, high):
        total = product(left[...], 0, g)
        for t in range(4):
            out[low:low + 4, 8 * t:8 * t + 8, lanes(g)] = total[8 * t:8 * t + 4]
            out[high:high + 4, 8 * t:8 * t + 8, lanes(g)] = total[8 * t + 4:8 * t + 8]

    def put1(left, g, low, high):
        total = product(left[...], 1, g)
        for t in range(2):
            part1[g, low:low + 4, 8 * t:8 * t + 8] = total[8 * t:8 * t + 4]
            part1[g, high:high + 4, 8 * t:8 * t + 8] = total[8 * t + 4:8 * t + 8]

    def inner_four(g):
        inner_rows(0, g, 4, wide0a, left0a)
        put0(left0a, g, 4, 8)
        inner_rows(0, g, 12, wide0b, left0b)
        put0(left0b, g, 12, 16)
        inner_rows(1, g, 4, wide1a, left1a)
        put1(left1a, g, 4, 8)
        inner_rows(0, g, 20, wide0c, left0c)

    def inner(g, carry):
        put0(left0c, g - 1, 20, 24)
        inner_four(g)
        return carry

    inner_four(0)
    start(zs, lambda way: [z_copy(way, 1, g) for g in range(GROUPS)], now)
    lax.fori_loop(1, GROUPS, inner, 0)
    put0(left0c, GROUPS - 1, 20, 24)

    for way in near:
        @pl.when(near[way])
        def _(way=way):
            pl.semaphore_wait(corner_ready, 1)
            if way == "xl":
                copies = [x_copy(way, g) for g in range(GROUPS)]
            else:
                copies = [z_copy(way, part, g) for part in range(2) for g in range(GROUPS)]
            for copy in copies:
                copy.start()

    def derive(g):
        for k in range(2):
            rows = z_in[g, 28 + 8 * k:36 + 8 * k].reshape(4, 2, 8, LANES)
            quad[k] = (rows[:, 0] + rows[:, 1]).reshape(32, LANES)
            means = 0.25 * (quad[k, pl.ds(0, 16, stride=2)] + quad[k, pl.ds(1, 16, stride=2)])
            for r in range(4):
                at, ring, odd = MIDDLE + 4 * k + r, RING + 2 * k + r // 2, r % 2
                halo[g, at, 0:2] = means[4 * r:4 * r + 2]
                halo[g, at, 6:8] = means[4 * r + 2:4 * r + 4]
                halo[g, at, 2:4] = z_in[g, ring, 2 * odd:2 * odd + 2]
                halo[g, at, 4:6] = z_in[g, ring, 4 + 2 * odd:6 + 2 * odd]

    def forward(g):
        arrived(zs, lambda way: [z_copy(way, 0, g)])
        start(xs, lambda way: [corner_copy(way, g)])

    def forward_first(g, carry):
        forward(g)
        return carry

    @pl.when(first)
    def _():
        lax.fori_loop(0, GROUPS, forward_first, 0)

    def outer(g, carry):
        arrived(xs, lambda way: [x_copy(way, g)])
        strips(g)
        outer_rows(0, g, wide0a, left0a)
        put0(left0a, g, 0, 28)
        outer_rows(1, g, wide1a, left1a)
        put1(left1a, g, 0, 12)
        outer_rows(2, g, wide2, left2)
        part2[g] = product(left2[...], 2, g)
        return carry

    def forward_then_outer(g, carry):
        @pl.when(jnp.logical_not(first) & (g < GROUPS))
        def _():
            forward(jnp.minimum(g, GROUPS - 1))

        return outer(g - 1, carry)

    @pl.when(jnp.logical_not(first))
    def _():
        forward(0)

    lax.fori_loop(1, GROUPS + 1, forward_then_outer, 0)

    groups = range(GROUPS)
    sent(xs, lambda way: [x_copy(way, g) for g in groups] + [corner_copy(way, g) for g in groups])
    sent(zs, lambda way: [z_copy(way, part, g) for part in range(2) for g in groups])

    first_row = (0, 32, 48)

    def edge_lines(level, g, unit):
        block = jnp.concatenate(
            [(z_in if near_z else halo)[g, at:at + 4] for near_z, at in UNITS[level][unit:unit + 3]], axis=0)
        lines = along_x(block, level, g)
        at = first_row[level] + 4 * unit
        twice[at:at + 4, 0:8] = lines
        twice[at:at + 4, 8:16] = lines
        added = line_sum([twice[at:at + 4, j:j + 8] for j in range(1, 8)],
                         [coef[level, g, j - 1] for j in range(1, 8)])
        split_into(left_edge, 8 * at, added)

    def edge(level, g):
        at = 8 * first_row[level]
        return product(left_edge[at:at + 8 * SIZES[level]], level, g)

    low8 = lax.broadcasted_iota(jnp.int32, (8, 8, LANES), 1) < HALF

    def edges(g, carry):
        arrived(zs, lambda way: [z_copy(way, 1, g)])
        for unit in range(1, 7):
            edge_lines(0, g, unit)
        derive(g)
        edge_lines(1, g, 1)
        edge_lines(1, g, 2)
        arrived(xs, lambda way: [corner_copy(way, g)])
        edge_lines(2, g, 0)
        edge_lines(2, g, 1)
        total2 = part2[g] + edge(2, g)
        up2[:, pl.ds(0, 8, stride=2)] = total2
        up2[:, pl.ds(1, 8, stride=2)] = total2
        edge_lines(1, g, 0)
        edge_lines(1, g, 3)
        edge1 = edge(1, g)
        for n in range(2):
            mine = edge1[8 * n:8 * n + 8]
            for t in range(2):
                coarse = up2[4 * n:4 * n + 4, 8 * t:8 * t + 8]
                both = jnp.broadcast_to(coarse[:, None], (4, 2, 8, LANES)).reshape(8, 8, LANES)
                side = jnp.where(low8, mine, 0.0) if t == 0 else jnp.where(low8, 0.0, mine)
                total1 = part1[g, 8 * n:8 * n + 8, 8 * t:8 * t + 8] + side + both
                up1[8 * n:8 * n + 8, pl.ds(16 * t, 8, stride=2)] = total1
                up1[8 * n:8 * n + 8, pl.ds(16 * t + 1, 8, stride=2)] = total1
        edge_lines(0, g, 0)
        edge_lines(0, g, 7)
        edge0 = edge(0, g)
        for n in range(4):
            mine = edge0[8 * n:8 * n + 8]
            for t in range(4):
                coarse = up1[4 * n:4 * n + 4, 8 * t:8 * t + 8]
                total = jnp.broadcast_to(coarse[:, None], (4, 2, 8, LANES)).reshape(8, 8, LANES)
                if t == 0:
                    total = total + jnp.where(low8, mine, 0.0)
                if t == 3:
                    total = total + jnp.where(low8, 0.0, mine)
                out[8 * n:8 * n + 8, 8 * t:8 * t + 8, lanes(g)] += total
        return carry

    lax.fori_loop(0, GROUPS, edges, 0)


def solution(mesh):
    nx, ny = mesh.shape["gx"], mesh.shape["gy"]
    hbm = pltpu.MemorySpace.HBM

    def body(field, vertical, horiz_kernel, gen_weight):
        def f32(*shape):
            return pltpu.VMEM(shape, F32)

        def bf16(rows):
            return pltpu.VMEM((rows, 2 * LANES), BF16)

        operands = (field, vertical, jnp.transpose(horiz_kernel, (0, 2, 1, 3)), gen_weight)
        return pl.pallas_call(
            functools.partial(kernel, nx, ny),
            out_shape=jax.ShapeDtypeStruct(field.shape, F32),
            in_specs=[pl.BlockSpec(memory_space=hbm)] * 4,
            out_specs=pl.BlockSpec(memory_space=pltpu.MemorySpace.VMEM),
            scratch_shapes=[
                f32(GROUPS, 32, 32, LANES), f32(GROUPS, 16, 16, LANES), f32(GROUPS, 8, 8, LANES),
                f32(2, GROUPS, STRIP[3], 8, LANES), f32(2, GROUPS, STRIP[3], 8, LANES),
                f32(GROUPS, 52, 8, LANES), f32(GROUPS, 52, 8, LANES), f32(GROUPS, ROWS, 8, LANES),
                f32(8, 48, LANES), f32(8, 48, LANES), f32(8, 48, LANES),
                f32(8, 32, LANES), f32(8, 24, LANES), f32(2, 4, 16, LANES), f32(2, 4, 8, LANES),
                f32(*vertical.shape), f32(GENS, VARS, 2, TAPS), f32(*gen_weight.shape),
                f32(GENS, GROUPS * LANES),
                f32(GENS, 2, GROUPS, TAPS, 8, LANES), f32(GENS, GROUPS, 7, 8, LANES),
                f32(LANES, LANES), pltpu.VMEM((GENS, GROUPS, 2 * LANES, 2 * LANES), BF16),
                f32(16, 32, LANES), f32(2, 32, LANES),
                bf16(256), bf16(256), bf16(256), bf16(128), bf16(64), f32(56, 16, LANES), bf16(448),
                f32(GROUPS, 16, 16, LANES), f32(GROUPS, 8, 8, LANES), f32(16, 32, LANES), f32(8, 16, LANES),
                pltpu.SemaphoreType.DMA((GROUPS + 3,)),
                pltpu.SemaphoreType.DMA((24,)),
                pltpu.SemaphoreType.DMA((24,)),
                pltpu.SemaphoreType.REGULAR,
            ],
            compiler_params=pltpu.CompilerParams(
                collective_id=0, has_side_effects=True, vmem_limit_bytes=40 * 2 ** 20),
        )(*[pltpu.with_memory_space_constraint(operand, hbm) for operand in operands])

    return jax.shard_map(
        body, mesh=mesh, in_specs=(P("gx", "gy", None), P(), P(), P()),
        out_specs=P("gx", "gy", None), check_vma=False)
```
